128 devices in a mesh: gx: 8 (over z, core), gy: 16 (over y, x).
Axes of the slice: x: 4, y: 4, z: 4, core: 2. Of those that a mesh axis runs over, the one named last changes fastest.
Arguments:
- charges: float32 [128, 256, 1024], P('gx', 'gy'), may hold values from -6 to 6
- kernel_taps: float32 [4, 3, 9], replicated, may hold values from 0.05 to 0.6
Outputs:
- potential: float32 [128, 256, 1024], P('gx', 'gy')
The draws below stay inside these ranges and needn't reach their ends.
All inputs are finite; a program needn't handle non-finite values.
Results may differ from the reference program's by a relative error of at most 0.00018.
Values sent between devices are 32-bit elements; how exact they have to be, the bound alone decides.
No kernel may reach another device: no remote copies, remote signals or barrier semaphores. Data moves between devices by JAX's collectives and lax.ppermute only.
A program may use at most 128 MiB of HBM per device.

```python
import jax
import jax.numpy as jnp
from jax import lax

NZ = 1024
NX = 128
NY = 256


def block_scale(own_key, shape, cuts, least, high):
    level, own = 1.0, jax.random.fold_in(own_key, 6)
    for position, blocks in cuts:
        steps = jnp.exp(jax.random.uniform(jax.random.fold_in(own, position), (blocks,), jnp.float32, least / len(cuts), high / len(cuts)))
        level = level * jnp.repeat(steps, shape[position] // blocks).reshape([-1 if axis == position else 1 for axis in range(len(shape))])
    return level


def normal_values(own_key, shape, scale, bound, cuts=(), dtype=jnp.bfloat16):
    drawn = jax.random.normal(own_key, shape, jnp.float32) * scale
    if len(cuts) > 0:
        drawn = block_scale(own_key, shape, cuts, -0.22, 0.18) * drawn
    return jnp.clip(drawn, min=-bound, max=bound).astype(dtype)


def setup_inputs(seed: int = 0) -> dict:
    key_of = jax.random.split(jax.random.key(seed), 3)
    charges = normal_values(key_of[0], (NX, NY, NZ), 1.0, 6.0, ((0, 8), (1, 16)), jnp.float32)
    kernel_taps = jnp.clip(jax.random.uniform(key_of[1], (4, 3, 9), jnp.float32, 0.05, 0.6), 0.05, 0.6)
    return {"charges": charges, "kernel_taps": kernel_taps}


stencil_weights = ((-3, -0.0625), (-1, 0.5625), (0, 1.0), (1, 0.5625), (3, -0.0625))


def convolve_along(values, kernel, along):
    summed = kernel[0] * jnp.roll(values, 4, along)
    for tap_index in range(1, 9):
        summed = summed + kernel[tap_index] * jnp.roll(values, 4 - tap_index, along)
    return summed


def convolve_three(values, kernel_rows):
    values = convolve_along(values, kernel_rows[0], 0)
    values = convolve_along(values, kernel_rows[1], 1)
    return convolve_along(values, kernel_rows[2], 2)


def restrict_along(values, along):
    length = values.shape[along]
    summed = None
    for offset, weight in stencil_weights:
        shifted = lax.slice_in_dim(jnp.roll(values, -offset, along), 0, length, 2, along)
        summed = weight * shifted if summed is None else summed + weight * shifted
    return summed


def restrict_three(values):
    return restrict_along(restrict_along(restrict_along(values, 0), 1), 2)


def prolong_padded(padded, along):
    length = padded.shape[along] - 4
    centre = lax.slice_in_dim(padded, 2, 2 + length, 1, along)
    right = lax.slice_in_dim(padded, 3, 3 + length, 1, along)
    left = lax.slice_in_dim(padded, 1, 1 + length, 1, along)
    farther = lax.slice_in_dim(padded, 4, 4 + length, 1, along)
    odd_cells = 0.5625 * (centre + right) - 0.0625 * (left + farther)
    stacked = jnp.stack([centre, odd_cells], axis=along + 1)
    new_shape = list(centre.shape)
    new_shape[along] = 2 * length
    return stacked.reshape(new_shape)


def prolong_along(values, along):
    widths = [(2, 2) if dim_index == along else (0, 0) for dim_index in range(3)]
    return prolong_padded(jnp.pad(values, widths, mode="wrap"), along)


def prolong_three(values):
    return prolong_along(prolong_along(prolong_along(values, 0), 1), 2)


def reference(charges, kernel_taps):
    grids = [charges]
    for section_index in range(3):
        grids.append(restrict_three(grids[section_index]))
    running = (0.5 ** 3) * convolve_three(grids[3], kernel_taps[3])
    for section_index in (2, 1, 0):
        running = (0.5 ** section_index) * convolve_three(grids[section_index], kernel_taps[section_index]) + prolong_three(running)
    return running
```

```python
import jax
import jax.numpy as jnp
import numpy as np
from jax import lax
from jax.experimental import pallas as pl
from jax.experimental.pallas import tpu as pltpu
from jax.sharding import PartitionSpec as P

first_cell = (0, -1, -2, -2)
cell_count = (16, 11, 9, 7)
brick_cells = (16, 8, 4, 2)
restrict_taps = {-3: -0.0625, -1: 0.5625, 0: 1.0, 1: 0.5625, 3: -0.0625}
lanes = 128
block_rows = ((), (0, 1, 2, 3), (4, 5), (6,))
rows_per_block = 8


def restrict_1d(level):
    matrix = np.zeros((cell_count[level + 1], cell_count[level]), np.float32)
    for coarse in range(cell_count[level + 1]):
        for fine in range(cell_count[level]):
            offset = first_cell[level] + fine - 2 * (first_cell[level + 1] + coarse)
            matrix[coarse, fine] = restrict_taps.get(offset, 0.0)
    return matrix


def prolong_entries(fine):
    if fine % 2 == 0:
        return {fine // 2: 1.0}
    left = (fine - 1) // 2
    return {left - 1: -0.0625, left: 0.5625, left + 1: 0.5625, left + 2: -0.0625}


def prolong_1d(level):
    matrix = np.zeros((cell_count[level], cell_count[level + 1]), np.float32)
    for fine in range(cell_count[level]):
        for coarse, weight in prolong_entries(first_cell[level] + fine).items():
            matrix[fine, coarse - first_cell[level + 1]] = weight
    return matrix


def padded(matrix, rows, columns):
    result = np.zeros((rows, columns), np.float32)
    result[: matrix.shape[0], : matrix.shape[1]] = matrix
    return jnp.asarray(result, jnp.bfloat16)


def restrict_window(rows, width, margin):
    matrix = np.zeros((rows, width), np.float32)
    for coarse in range(rows):
        for offset, weight in restrict_taps.items():
            matrix[coarse, margin + 2 * coarse + offset] = weight
    return jnp.asarray(matrix, jnp.bfloat16)


def prolong_window(rows, width, margin):
    matrix = np.zeros((rows, width), np.float32)
    for fine in range(rows):
        for coarse, weight in prolong_entries(fine).items():
            matrix[fine, margin + coarse] = weight
    return jnp.asarray(matrix, jnp.bfloat16)


def tap_bases():
    bases = np.full((6, lanes, lanes), 256, np.int32)
    for level in (1, 2, 3):
        count = cell_count[level]
        for axis in (0, 1):
            for source in range(count * count):
                for wanted in range(count * count):
                    here, there = divmod(source, count), divmod(wanted, count)
                    if here[1 - axis] == there[1 - axis]:
                        bases[2 * (level - 1) + axis, source, wanted] = here[axis] - there[axis] + 4
    return jnp.asarray(bases)


def brick_offsets(level, axis, bricks):
    if level == 3 and axis == 0:
        return tuple(range(bricks))
    reach = {1: 1, 2: 3, 3: 5}[level]
    return tuple(range(-reach, reach + 1))


def weight_sections(count_x, count_y):
    sections, start = {}, 0
    for level in (1, 2, 3):
        for axis, bricks in ((0, count_x), (1, count_y)):
            offsets = brick_offsets(level, axis, bricks)
            sections[level, axis] = (start, offsets)
            start += len(offsets)
    return sections, start


def split(values):
    high = values.astype(jnp.bfloat16)
    return high, (values - high.astype(jnp.float32)).astype(jnp.bfloat16)


def dot(left, right):
    return lax.dot_general(left, right, (((1,), (0,)), ((), ())), preferred_element_type=jnp.float32)


def dot_lanes(left, right):
    return lax.dot_general(left, right, (((1,), (1,)), ((), ())), preferred_element_type=jnp.float32)


def wrapped(values, margin, axis):
    size = values.shape[axis]
    tail = lax.slice_in_dim(values, size - margin, size, axis=axis)
    head = lax.slice_in_dim(values, 0, margin, axis=axis)
    return jnp.concatenate([tail, values, head], axis=axis)


def restrict_kernel(taps, charges, down_1, down_2, down_3, lane_window, row_window, blocks, rim):
    rows_x, rows_y, depth = charges.shape
    high, low = split(charges[...].reshape(rows_x * rows_y, depth))
    patch = dot(down_1[...], high) + dot(down_1[...], low)
    high, low = split(wrapped(patch, lanes, 1))
    pieces = []
    for begin in range(0, depth, 256):
        pieces.append(
            dot_lanes(lane_window[...], high[:, begin : begin + 512])
            + dot_lanes(lane_window[...], low[:, begin : begin + 512])
        )
    grid = jnp.concatenate(pieces, axis=0)
    for level in (1, 2, 3):
        cells = grid.shape[0]
        rim[0:8, :] = grid[cells - 8 :, :]
        rim[8 : 8 + cells, :] = grid
        rim[8 + cells : 16 + cells, :] = grid[:8, :]
        for index, row in enumerate(block_rows[level]):
            summed = None
            for tap in range(9):
                begin = lanes * index + 4 + tap
                term = taps[3 * level + 2, tap] * rim[begin : begin + lanes, :]
                summed = term if summed is None else summed + term
            blocks[pl.ds(row, lanes, stride=rows_per_block), :] = summed
        if level == 3:
            break
        down = down_2 if level == 1 else down_3
        high, low = split(grid)
        high, low = split(wrapped(dot(high, down[...]) + dot(low, down[...]), 64, 0))
        pieces = []
        for begin in range(0, cells, 256):
            pieces.append(
                dot(row_window[...], high[begin : begin + 384])
                + dot(row_window[...], low[begin : begin + 384])
            )
        grid = jnp.concatenate(pieces, axis=0)
    blocks[pl.ds(7, lanes, stride=rows_per_block), :] = jnp.zeros((lanes, lanes), jnp.float32)


def weight_kernel(sections, taps, bases, weights):
    for (level, axis), (start, offsets) in sections.items():
        base = bases[2 * (level - 1) + axis]
        scale = 0.5**level if axis == 0 else 1.0
        values = [scale * taps[3 * level + axis, tap] for tap in range(9)]
        for index, offset in enumerate(offsets):
            number = base + brick_cells[level] * offset
            if level == 3 and axis == 0:
                number = number & 271
            chosen = jnp.zeros((lanes, lanes), jnp.float32)
            for tap in range(9):
                chosen = jnp.where(number == tap, values[tap], chosen)
            high, low = split(chosen)
            begin = (start + index) * lanes
            weights[begin : begin + lanes, 0:lanes] = high
            weights[begin : begin + lanes, lanes : 2 * lanes] = low


def weighted(pieces, weights, start):
    high = jnp.concatenate([piece[0] for piece in pieces], axis=1)
    low = jnp.concatenate([piece[1] for piece in pieces], axis=1)
    rows = pl.ds(start * lanes, len(pieces) * lanes)
    both = dot(high, weights[rows, :])
    return both[:, :lanes] + both[:, lanes:] + dot(low, weights[rows, 0:lanes])


def convolve_kernel(sections, count_x, count_y, received, weights, blocks):
    for level in (1, 2, 3):
        slices = len(block_rows[level])
        values = jnp.concatenate(
            [received[pl.ds(row, lanes, stride=rows_per_block), :] for row in block_rows[level]], axis=0
        )
        start, offsets = sections[level, 0]
        parts = [part.reshape(slices, count_x, count_y, lanes) for part in split(values)]
        pieces = []
        for offset in offsets:
            turn = offset % count_x
            pieces.append(
                [
                    jnp.concatenate([part[:, turn:], part[:, :turn]], axis=1).reshape(slices * lanes, lanes)
                    if turn
                    else part.reshape(slices * lanes, lanes)
                    for part in parts
                ]
            )
        values = weighted(pieces, weights, start)
        start, offsets = sections[level, 1]
        stack = values.reshape(slices * count_x, count_y, lanes)
        pieces = []
        for offset in offsets:
            turn = offset % count_y
            turned = jnp.concatenate([stack[:, turn:], stack[:, :turn]], axis=1) if turn else stack
            pieces.append(split(turned.reshape(slices * lanes, lanes)))
        values = weighted(pieces, weights, start)
        for index, row in enumerate(block_rows[level]):
            blocks[pl.ds(row, lanes, stride=rows_per_block), :] = values[lanes * index : lanes * (index + 1)]
    blocks[pl.ds(7, lanes, stride=rows_per_block), :] = jnp.zeros((lanes, lanes), jnp.float32)


def prolong_rows(values, row_window):
    high, low = split(wrapped(values, 64, 0))
    pieces = []
    for begin in range(0, values.shape[0], lanes):
        pieces.append(
            dot(row_window[...], high[begin : begin + 256]) + dot(row_window[...], low[begin : begin + 256])
        )
    return jnp.concatenate(pieces, axis=0)


def finish_kernel(received, up_3, up_2, up_1, row_window, finest, potential):
    running = received[pl.ds(block_rows[3][0], lanes, stride=rows_per_block), :]
    for level, up in ((2, up_3), (1, up_2)):
        own = jnp.concatenate(
            [received[pl.ds(row, lanes, stride=rows_per_block), :] for row in block_rows[level]], axis=0
        )
        high, low = split(running)
        running = own + prolong_rows(dot(high, up[...]) + dot(low, up[...]), row_window)
    high, low = split(prolong_rows(running, row_window))
    smooth = dot_lanes(up_1[...], high) + dot_lanes(up_1[...], low)
    potential[...] = finest[...] + smooth.reshape(potential.shape)


def convolve_x_kernel(taps, before, own, after, summed_ref, head, tail):
    rows_x, rows_y, depth = own.shape

    def layer(index):
        if index < 4:
            return before[index]
        return own[index - 4] if index < 4 + rows_x else after[index - 4 - rows_x]

    for row in range(rows_x):
        summed = taps[0, 0] * layer(row)
        for tap in range(1, 9):
            summed = summed + taps[0, tap] * layer(row + tap)
        summed_ref[row] = summed
        head[row] = summed[:4]
        tail[row] = summed[rows_y - 4 :]


def convolve_yz_kernel(taps, before, own, after, result, rim):
    rows_x, rows_y, depth = own.shape
    for row in range(rows_x):
        rim[row, 4:8, :] = before[row]
        rim[row, 8 : 8 + rows_y, :] = own[row]
        rim[row, 8 + rows_y : 12 + rows_y, :] = after[row]
    for row in range(rows_x):
        summed = taps[1, 0] * rim[row, 4 : 4 + rows_y, :]
        for tap in range(1, 9):
            summed = summed + taps[1, tap] * rim[row, 4 + tap : 4 + tap + rows_y, :]
        total = taps[2, 4] * summed
        for tap in (0, 1, 2, 3, 5, 6, 7, 8):
            total = total + taps[2, tap] * pltpu.roll(summed, (4 - tap) % depth, 1)
        result[row] = total


def in_vmem(count):
    return [pl.BlockSpec(memory_space=pltpu.VMEM)] * count


scalars = pl.BlockSpec(memory_space=pltpu.SMEM)


def shape_of(*shape, dtype=jnp.float32):
    return jax.ShapeDtypeStruct(shape, dtype)


def call(kernel, outs, in_specs, scratch=(), flops=0, moved=0):
    return pl.pallas_call(
        kernel,
        out_shape=outs,
        in_specs=in_specs,
        out_specs=jax.tree.map(lambda _: pl.BlockSpec(memory_space=pltpu.VMEM), outs),
        scratch_shapes=list(scratch),
        compiler_params=pltpu.CompilerParams(vmem_limit_bytes=40 * 2**20),
        cost_estimate=pl.CostEstimate(flops=flops, bytes_accessed=moved, transcendentals=0),
    )


def per_device(charges, kernel_taps):
    count_x, count_y = lax.axis_size("gx"), lax.axis_size("gy")
    rows_x, rows_y, depth = charges.shape
    taps = kernel_taps.reshape(12, 9)
    both = ("gx", "gy")
    downs = [restrict_1d(level) for level in range(3)]
    ups = [prolong_1d(level) for level in range(3)]
    down_1 = padded(np.kron(downs[0], downs[0]), lanes, rows_x * rows_y)
    down_2 = padded(np.kron(downs[1].T, downs[1].T), lanes, lanes)
    down_3 = padded(np.kron(downs[2].T, downs[2].T), lanes, lanes)
    up_1 = padded(np.kron(ups[0], ups[0]), rows_x * rows_y, lanes)
    up_2 = padded(np.kron(ups[1].T, ups[1].T), lanes, lanes)
    up_3 = padded(np.kron(ups[2].T, ups[2].T), lanes, lanes)
    sections, section_count = weight_sections(count_x, count_y)
    block_shape = (lanes * rows_per_block, lanes)
    exchange_shape = (lanes, rows_per_block, lanes)

    blocks = call(
        restrict_kernel,
        shape_of(*block_shape),
        [scalars] + in_vmem(6),
        [pltpu.VMEM((depth // 2 + 16, lanes), jnp.float32)],
        flops=10**9,
        moved=2 * 10**6,
    )(
        taps,
        charges,
        down_1,
        down_2,
        down_3,
        restrict_window(lanes, 512, 128),
        restrict_window(lanes, 384, 64),
    )
    received = lax.all_to_all(blocks.reshape(exchange_shape), both, 0, 0, tiled=True)

    weights = call(
        lambda *refs: weight_kernel(sections, *refs),
        shape_of(section_count * lanes, 2 * lanes, dtype=jnp.bfloat16),
        [scalars] + in_vmem(1),
        flops=2 * 10**7,
        moved=3 * 10**6,
    )(taps, tap_bases())

    def shifted(values, axis, step):
        count = lax.axis_size(axis)
        return lax.ppermute(values, axis, [(i, (i + step) % count) for i in range(count)])

    before = shifted(charges[rows_x - 4 :], "gx", 1)
    after = shifted(charges[:4], "gx", -1)
    summed, head, tail = call(
        convolve_x_kernel,
        (shape_of(rows_x, rows_y, depth), shape_of(rows_x, 4, depth), shape_of(rows_x, 4, depth)),
        [scalars] + in_vmem(3),
        flops=18 * rows_x * rows_y * depth,
        moved=3 * 10**6,
    )(taps, before, charges, after)
    finest = call(
        convolve_yz_kernel,
        shape_of(rows_x, rows_y, depth),
        [scalars] + in_vmem(3),
        [pltpu.VMEM((rows_x, rows_y + 16, depth), jnp.float32)],
        flops=36 * rows_x * rows_y * depth,
        moved=3 * 10**6,
    )(taps, shifted(tail, "gy", 1), summed, shifted(head, "gy", -1))

    blocks = call(
        lambda *refs: convolve_kernel(sections, count_x, count_y, *refs),
        shape_of(*block_shape),
        in_vmem(2),
        flops=10**9,
        moved=4 * 10**6,
    )(received.reshape(block_shape), weights)
    received = lax.all_to_all(blocks.reshape(exchange_shape), both, 0, 0, tiled=True)

    return call(
        finish_kernel,
        shape_of(rows_x, rows_y, depth),
        in_vmem(6),
        flops=10**9,
        moved=4 * 10**6,
    )(received.reshape(block_shape), up_3, up_2, up_1, prolong_window(256, 256, 64), finest)


def solution(mesh):
    placed = (P("gx", "gy", None), P())
    return jax.shard_map(
        per_device, mesh=mesh, in_specs=placed, out_specs=P("gx", "gy", None), check_vma=False
    )
```

```python
import jax
import jax.numpy as jnp
import numpy as np
from jax import lax
from jax.experimental import pallas as pl
from jax.experimental.pallas import tpu as pltpu
from jax.sharding import PartitionSpec as P

first_cell = (0, -1, -2, -2)
cell_count = (16, 11, 9, 7)
brick_cells = (16, 8, 4, 2)
restrict_taps = {-3: -0.0625, -1: 0.5625, 0: 1.0, 1: 0.5625, 3: -0.0625}
lanes = 128
block_rows = ((), (0, 1, 2, 3), (4, 5), (6,))
rows_per_block = 8


def restrict_1d(level):
    matrix = np.zeros((cell_count[level + 1], cell_count[level]), np.float32)
    for coarse in range(cell_count[level + 1]):
        for fine in range(cell_count[level]):
            offset = first_cell[level] + fine - 2 * (first_cell[level + 1] + coarse)
            matrix[coarse, fine] = restrict_taps.get(offset, 0.0)
    return matrix


def prolong_entries(fine):
    if fine % 2 == 0:
        return {fine // 2: 1.0}
    left = (fine - 1) // 2
    return {left - 1: -0.0625, left: 0.5625, left + 1: 0.5625, left + 2: -0.0625}


def prolong_1d(level):
    matrix = np.zeros((cell_count[level], cell_count[level + 1]), np.float32)
    for fine in range(cell_count[level]):
        for coarse, weight in prolong_entries(first_cell[level] + fine).items():
            matrix[fine, coarse - first_cell[level + 1]] = weight
    return matrix


def padded(matrix, rows, columns):
    result = np.zeros((rows, columns), np.float32)
    result[: matrix.shape[0], : matrix.shape[1]] = matrix
    return result


def restrict_window(rows, width, margin):
    matrix = np.zeros((rows, width), np.float32)
    for coarse in range(rows):
        for offset, weight in restrict_taps.items():
            matrix[coarse, margin + 2 * coarse + offset] = weight
    return matrix


def prolong_window(rows, width, margin):
    matrix = np.zeros((rows, width), np.float32)
    for fine in range(rows):
        for coarse, weight in prolong_entries(fine).items():
            matrix[fine, margin + coarse] = weight
    return matrix


def tap_tables():
    tables = []
    for level in (1, 2, 3):
        count = cell_count[level]
        for axis in (0, 1):
            chooser, same, number = (np.zeros((rows, lanes), np.float32) for rows in (lanes, lanes, 16))
            number[:] = 256.0
            for cell in range(count * count):
                place = divmod(cell, count)
                chooser[cell, place[axis]] = 1.0
                for other in range(count * count):
                    same[cell, other] = divmod(other, count)[1 - axis] == place[1 - axis]
                for source in range(count):
                    number[source, cell] = source - place[axis] + 4
            tables += [chooser, same, number]
    return jnp.asarray(np.concatenate(tables), jnp.bfloat16)


def brick_offsets(level, axis, bricks):
    if level == 3 and axis == 0:
        return tuple(range(bricks))
    reach = {1: 1, 2: 3, 3: 5}[level]
    return tuple(range(-reach, reach + 1))


def weight_sections(count_x, count_y):
    sections, start = {}, 0
    for level in (1, 2, 3):
        for axis, bricks in ((0, count_x), (1, count_y)):
            offsets = brick_offsets(level, axis, bricks)
            sections[level, axis] = (start, offsets)
            start += len(offsets)
    return sections, start


def split(values):
    high = values.astype(jnp.bfloat16)
    return high, (values - high.astype(jnp.float32)).astype(jnp.bfloat16)


def dot(left, right):
    return lax.dot_general(left, right, (((1,), (0,)), ((), ())), preferred_element_type=jnp.float32)


def dot_lanes(left, right):
    return lax.dot_general(left, right, (((1,), (1,)), ((), ())), preferred_element_type=jnp.float32)


def wrapped(values, margin, axis):
    size = values.shape[axis]
    tail = lax.slice_in_dim(values, size - margin, size, axis=axis)
    head = lax.slice_in_dim(values, 0, margin, axis=axis)
    return jnp.concatenate([tail, values, head], axis=axis)


def both_ways(product):
    half = product.shape[1] // 2
    return product[:, :half] + product[:, half:]


def side_by_side(values):
    return jnp.concatenate(split(values), axis=1)


def restrict_kernel(
    taps_far, charges_far, constants_far, blocks_far, head, tail, taps, charges, constants, patch, rim, blocks, arrived
):
    rows_x, rows_y, depth = charges.shape
    columns = rows_x * rows_y
    copies = [
        pltpu.make_async_copy(constants_far, constants, arrived.at[0]),
        pltpu.make_async_copy(taps_far, taps, arrived.at[1]),
    ]
    leaving = [
        pltpu.make_async_copy(charges.at[pl.ds(0, 4)], head, arrived.at[2]),
        pltpu.make_async_copy(charges.at[pl.ds(rows_x - 4, 4)], tail, arrived.at[3]),
    ]
    chunks = []
    for index in range(depth // 256):
        section = pl.ds(256 * index, 256)
        chunks.append(
            pltpu.make_async_copy(
                charges_far.at[:, :, section], charges.at[:, :, section], arrived.at[4 + index]
            )
        )
    copies[0].start()
    for chunk in chunks:
        chunk.start()
    copies[1].start()
    copies[0].wait()
    for index, chunk in enumerate(chunks):
        chunk.wait()
        high, low = split(charges[:, :, 256 * index : 256 * (index + 1)].reshape(columns, 256))
        down = constants[:, 0:columns]
        high, low = split(dot(down, high) + dot(down, low))
        begin = lanes + 256 * index
        patch[0:lanes, begin : begin + 256] = high
        patch[lanes : 2 * lanes, begin : begin + 256] = low
    for copy in leaving:
        copy.start()
    patch[:, 0:lanes] = patch[:, depth : depth + lanes]
    patch[:, depth + lanes : depth + 2 * lanes] = patch[:, lanes : 2 * lanes]
    lane_window = constants[:, 256:768]
    row_window = constants[:, 768:1152]
    grid = jnp.concatenate(
        [
            both_ways(dot_lanes(lane_window, patch[:, begin : begin + 512]))
            for begin in range(0, depth, 256)
        ],
        axis=0,
    )
    copies[1].wait()
    for level in (1, 2, 3):
        cells = grid.shape[0]
        rim[0:8, :] = grid[cells - 8 :, :]
        rim[8 : 8 + cells, :] = grid
        rim[8 + cells : 16 + cells, :] = grid[:8, :]
        for index, row in enumerate(block_rows[level]):
            summed = None
            for tap in range(9):
                begin = lanes * index + 4 + tap
                term = taps[2, level, tap] * rim[begin : begin + lanes, :]
                summed = term if summed is None else summed + term
            blocks[pl.ds(row, lanes, stride=rows_per_block), :] = summed
        if level == 3:
            break
        down = constants[:, 1024 + 128 * level : 1152 + 128 * level]
        grid = dot(side_by_side(grid), jnp.concatenate([down, down], axis=0))
        ready = wrapped(side_by_side(grid), 64, 0)
        grid = jnp.concatenate(
            [both_ways(dot(row_window, ready[begin : begin + 384])) for begin in range(0, cells, 256)], axis=0
        )
    blocks[pl.ds(7, lanes, stride=rows_per_block), :] = jnp.zeros((lanes, lanes), jnp.float32)
    for index in range(4):
        section = pl.ds(256 * index, 256)
        leaving.append(
            pltpu.make_async_copy(blocks.at[section], blocks_far.at[section], arrived.at[4 + depth // 256 + index])
        )
        leaving[-1].start()
    for copy in leaving:
        copy.wait()


def weight_kernel(sections, taps, tables, weights):
    for (level, axis), (start, offsets) in sections.items():
        begin = (2 * (level - 1) + axis) * (2 * lanes + 16)
        chooser = tables[begin : begin + lanes, 0:16]
        same = tables[begin + lanes : begin + 2 * lanes, :]
        base = tables[begin + 2 * lanes : begin + 2 * lanes + 16, :].astype(jnp.float32).astype(jnp.int32)
        scale = 0.5**level if axis == 0 else 1.0
        values = [scale * taps[axis, level, tap] for tap in range(9)]
        for index, offset in enumerate(offsets):
            number = base + brick_cells[level] * offset
            if level == 3 and axis == 0:
                number = number & 271
            chosen = jnp.zeros(number.shape, jnp.float32)
            for tap in range(9):
                chosen = jnp.where(number == tap, values[tap], chosen)
            spread = dot(chooser, side_by_side(chosen)).astype(jnp.bfloat16)
            rows = pl.ds((start + index) * lanes, lanes)
            weights[rows, 0:lanes] = spread[:, :lanes] * same
            weights[rows, lanes : 2 * lanes] = spread[:, lanes:] * same


def weighted(pieces, weights, start):
    rows = pl.ds(start * lanes, len(pieces) * lanes)
    product = both_ways(dot(jnp.concatenate(pieces, axis=1), weights[rows, :]))
    half = product.shape[0] // 2
    return product[:half] + product[half:]


def convolve_kernel(sections, count_x, count_y, received, weights, blocks):
    for level in (1, 2, 3):
        slices = len(block_rows[level])
        values = jnp.concatenate(
            [received[pl.ds(row, lanes, stride=rows_per_block), :] for row in block_rows[level]], axis=0
        )
        start, offsets = sections[level, 0]
        stack = jnp.concatenate(split(values), axis=0).reshape(2 * slices, count_x, count_y, lanes)
        pieces = []
        for offset in offsets:
            turn = offset % count_x
            turned = jnp.concatenate([stack[:, turn:], stack[:, :turn]], axis=1) if turn else stack
            pieces.append(turned.reshape(2 * slices * lanes, lanes))
        values = weighted(pieces, weights, start)
        start, offsets = sections[level, 1]
        stack = values.reshape(slices * count_x, count_y, lanes)
        pieces = []
        for offset in offsets:
            turn = offset % count_y
            turned = jnp.concatenate([stack[:, turn:], stack[:, :turn]], axis=1) if turn else stack
            pieces.append(jnp.concatenate(split(turned.reshape(slices * lanes, lanes)), axis=0))
        values = weighted(pieces, weights, start)
        for index, row in enumerate(block_rows[level]):
            blocks[pl.ds(row, lanes, stride=rows_per_block), :] = values[lanes * index : lanes * (index + 1)]
    blocks[pl.ds(7, lanes, stride=rows_per_block), :] = jnp.zeros((lanes, lanes), jnp.float32)


def finish_kernel(received, constants, finest, potential, ready, left):
    rows_x, rows_y, depth = finest.shape
    row_window = constants[:, 512:768]
    running = received[pl.ds(block_rows[3][0], lanes, stride=rows_per_block), :]
    for level in (2, 1):
        own = jnp.concatenate(
            [received[pl.ds(row, lanes, stride=rows_per_block), :] for row in block_rows[level]], axis=0
        )
        up = constants[:, 128 * (2 - level) : 128 * (3 - level)]
        pairs = wrapped(side_by_side(dot(side_by_side(running), up)), 64, 0)
        running = own + jnp.concatenate(
            [
                both_ways(dot(row_window, pairs[begin : begin + 256]))
                for begin in range(0, running.shape[0], lanes)
            ],
            axis=0,
        )
    pairs = wrapped(side_by_side(running), 64, 0)
    copies = []
    for index in range(depth // 256):
        fine = both_ways(dot(row_window, pairs[lanes * index : lanes * index + 256]))
        smooth = dot_lanes(constants[:, 256:512], side_by_side(fine))
        section = slice(256 * index, 256 * (index + 1))
        ready[:, :, section] = finest[:, :, section] + smooth.reshape(rows_x, rows_y, 256)
        places = pl.ds(256 * index, 256)
        copies.append(
            pltpu.make_async_copy(ready.at[:, :, places], potential.at[:, :, places], left.at[index])
        )
        copies[-1].start()
    for copy in copies:
        copy.wait()


def convolve_x_kernel(taps, before, own, after, summed_ref, head, tail):
    rows_x, rows_y, depth = own.shape

    def layer(index):
        if index < 4:
            return before[index]
        return own[index - 4] if index < 4 + rows_x else after[index - 4 - rows_x]

    for row in range(rows_x):
        summed = taps[0, 0, 0] * layer(row)
        for tap in range(1, 9):
            summed = summed + taps[0, 0, tap] * layer(row + tap)
        summed_ref[row] = summed
        head[row] = summed[:4]
        tail[row] = summed[rows_y - 4 :]


def convolve_yz_kernel(taps, before, own, after, result, rim):
    rows_x, rows_y, depth = own.shape
    for row in range(rows_x):
        rim[row, 4:8, :] = before[row]
        rim[row, 8 : 8 + rows_y, :] = own[row]
        rim[row, 8 + rows_y : 12 + rows_y, :] = after[row]
    for row in range(rows_x):
        summed = taps[1, 0, 0] * rim[row, 4 : 4 + rows_y, :]
        for tap in range(1, 9):
            summed = summed + taps[1, 0, tap] * rim[row, 4 + tap : 4 + tap + rows_y, :]
        total = taps[2, 0, 4] * summed
        for tap in (0, 1, 2, 3, 5, 6, 7, 8):
            total = total + taps[2, 0, tap] * pltpu.roll(summed, (4 - tap) % depth, 1)
        result[row] = total


def in_vmem(count):
    return [pl.BlockSpec(memory_space=pltpu.VMEM)] * count


scalars = pl.BlockSpec(memory_space=pltpu.SMEM)
far = pl.BlockSpec(memory_space=pltpu.HBM)


def shape_of(*shape, dtype=jnp.float32):
    return jax.ShapeDtypeStruct(shape, dtype)


def call(kernel, outs, in_specs, scratch=(), out_specs=None, limit=16, flops=0, moved=0):
    if out_specs is None:
        out_specs = jax.tree.map(lambda _: pl.BlockSpec(memory_space=pltpu.VMEM), outs)
    return pl.pallas_call(
        kernel,
        out_shape=outs,
        in_specs=in_specs,
        out_specs=out_specs,
        scratch_shapes=list(scratch),
        compiler_params=pltpu.CompilerParams(vmem_limit_bytes=limit * 2**20),
        cost_estimate=pl.CostEstimate(flops=flops, bytes_accessed=moved, transcendentals=0),
    )


def per_device(charges, kernel_taps):
    count_x, count_y = lax.axis_size("gx"), lax.axis_size("gy")
    rows_x, rows_y, depth = charges.shape
    taps = jnp.transpose(kernel_taps, (1, 0, 2))
    both = ("gx", "gy")
    downs = [restrict_1d(level) for level in range(3)]
    ups = [prolong_1d(level) for level in range(3)]
    down_constants = np.concatenate(
        [
            padded(np.kron(downs[0], downs[0]), lanes, rows_x * rows_y),
            restrict_window(lanes, 512, 128),
            restrict_window(lanes, 384, 64),
            padded(np.kron(downs[1].T, downs[1].T), lanes, lanes),
            padded(np.kron(downs[2].T, downs[2].T), lanes, lanes),
        ],
        axis=1,
    )
    down_constants = jnp.asarray(down_constants, jnp.bfloat16)

    def twice(matrix, axis):
        return np.concatenate([matrix, matrix], axis=axis)

    up_1, up_2, up_3 = (
        padded(matrix, rows, lanes)
        for matrix, rows in (
            (np.kron(ups[0], ups[0]), 256),
            (np.kron(ups[1].T, ups[1].T), lanes),
            (np.kron(ups[2].T, ups[2].T), lanes),
        )
    )
    up_constants = jnp.asarray(
        np.concatenate(
            [twice(up_3, 0), twice(up_2, 0), twice(up_1, 1), prolong_window(256, 256, 64)], axis=1
        ),
        jnp.bfloat16,
    )
    sections, section_count = weight_sections(count_x, count_y)
    block_shape = (lanes * rows_per_block, lanes)
    exchange_shape = (lanes, rows_per_block, lanes)

    blocks, head, tail = call(
        restrict_kernel,
        (
            shape_of(*block_shape),
            shape_of(4, rows_y, depth),
            shape_of(4, rows_y, depth),
        ),
        [far] * 3,
        [
            pltpu.SMEM(taps.shape, jnp.float32),
            pltpu.VMEM((rows_x, rows_y, depth), jnp.float32),
            pltpu.VMEM(down_constants.shape, jnp.bfloat16),
            pltpu.VMEM((2 * lanes, depth + 2 * lanes), jnp.bfloat16),
            pltpu.VMEM((depth // 2 + 16, lanes), jnp.float32),
            pltpu.VMEM(block_shape, jnp.float32),
            pltpu.SemaphoreType.DMA((8 + depth // 256,)),
        ],
        (far,) * 3,
        limit=60,
        flops=10**9,
        moved=2 * 10**6,
    )(taps, charges, down_constants)
    received = lax.all_to_all(blocks.reshape(exchange_shape), both, 0, 0, tiled=True)

    weights = call(
        lambda *refs: weight_kernel(sections, *refs),
        shape_of(section_count * lanes, 2 * lanes, dtype=jnp.bfloat16),
        [scalars] + in_vmem(1),
        flops=2 * 10**7,
        moved=3 * 10**6,
    )(taps, tap_tables())

    def shifted(values, axis, step):
        count = lax.axis_size(axis)
        return lax.ppermute(values, axis, [(i, (i + step) % count) for i in range(count)])

    before = shifted(tail, "gx", 1)
    after = shifted(head, "gx", -1)
    summed, head, tail = call(
        convolve_x_kernel,
        (shape_of(rows_x, rows_y, depth), shape_of(rows_x, 4, depth), shape_of(rows_x, 4, depth)),
        [scalars] + in_vmem(3),
        flops=10**11,
        moved=3 * 10**6,
    )(taps, before, charges, after)
    received, _ = lax.optimization_barrier((received, tail))
    finest = call(
        convolve_yz_kernel,
        shape_of(rows_x, rows_y, depth),
        [scalars] + in_vmem(3),
        [pltpu.VMEM((rows_x, rows_y + 16, depth), jnp.float32)],
        flops=10**11,
        moved=3 * 10**6,
    )(taps, shifted(tail, "gy", 1), summed, shifted(head, "gy", -1))

    blocks = call(
        lambda *refs: convolve_kernel(sections, count_x, count_y, *refs),
        shape_of(*block_shape),
        in_vmem(2),
        flops=10**9,
        moved=4 * 10**6,
    )(received.reshape(block_shape), weights)
    received = lax.all_to_all(blocks.reshape(exchange_shape), both, 0, 0, tiled=True)

    return call(
        finish_kernel,
        shape_of(rows_x, rows_y, depth),
        in_vmem(3),
        [pltpu.VMEM((rows_x, rows_y, depth), jnp.float32), pltpu.SemaphoreType.DMA((depth // 256,))],
        far,
        flops=10**9,
        moved=4 * 10**6,
    )(received.reshape(block_shape), up_constants, finest)


def solution(mesh):
    placed = (P("gx", "gy", None), P())
    return jax.shard_map(
        per_device, mesh=mesh, in_specs=placed, out_specs=P("gx", "gy", None), check_vma=False
    )
```

```python
import jax
import jax.numpy as jnp
import numpy as np
from jax import lax
from jax.experimental import pallas as pl
from jax.experimental.pallas import tpu as pltpu
from jax.sharding import PartitionSpec as P

first_cell = (0, -1, -2, -2)
cell_count = (16, 11, 9, 7)
brick_cells = (16, 8, 4, 2)
restrict_taps = {-3: -0.0625, -1: 0.5625, 0: 1.0, 1: 0.5625, 3: -0.0625}
lanes = 128
block_rows = ((), (0, 1, 2, 3), (4, 5), (6,))
rows_per_block = 7


def restrict_1d(level):
    matrix = np.zeros((cell_count[level + 1], cell_count[level]), np.float32)
    for coarse in range(cell_count[level + 1]):
        for fine in range(cell_count[level]):
            offset = first_cell[level] + fine - 2 * (first_cell[level + 1] + coarse)
            matrix[coarse, fine] = restrict_taps.get(offset, 0.0)
    return matrix


def prolong_entries(fine):
    if fine % 2 == 0:
        return {fine // 2: 1.0}
    left = (fine - 1) // 2
    return {left - 1: -0.0625, left: 0.5625, left + 1: 0.5625, left + 2: -0.0625}


def prolong_1d(level):
    matrix = np.zeros((cell_count[level], cell_count[level + 1]), np.float32)
    for fine in range(cell_count[level]):
        for coarse, weight in prolong_entries(first_cell[level] + fine).items():
            matrix[fine, coarse - first_cell[level + 1]] = weight
    return matrix


def padded(matrix, rows, columns):
    result = np.zeros((rows, columns), np.float32)
    result[: matrix.shape[0], : matrix.shape[1]] = matrix
    return result


def restrict_window(rows, width, margin):
    matrix = np.zeros((rows, width), np.float32)
    for coarse in range(rows):
        for offset, weight in restrict_taps.items():
            matrix[coarse, margin + 2 * coarse + offset] = weight
    return matrix


def prolong_window(rows, width, margin):
    matrix = np.zeros((rows, width), np.float32)
    for fine in range(rows):
        for coarse, weight in prolong_entries(fine).items():
            matrix[fine, margin + coarse] = weight
    return matrix


def prolong_ring(rows):
    matrix = np.zeros((rows, rows // 2), np.float32)
    for fine in range(rows):
        for coarse, weight in prolong_entries(fine).items():
            matrix[fine, coarse % (rows // 2)] = weight
    return matrix


def tap_tables():
    tables = []
    for level in (1, 2, 3):
        count = cell_count[level]
        for axis in (0, 1):
            chooser, same, number = (np.zeros((rows, lanes), np.float32) for rows in (lanes, lanes, 16))
            number[:] = 256.0
            for cell in range(count * count):
                place = divmod(cell, count)
                chooser[cell, place[axis]] = 1.0
                for other in range(count * count):
                    same[cell, other] = divmod(other, count)[1 - axis] == place[1 - axis]
                for source in range(count):
                    number[source, cell] = source - place[axis] + 4
            tables += [chooser, same, number]
    return jnp.asarray(np.concatenate(tables), jnp.bfloat16)


def brick_offsets(level, axis, bricks):
    if level == 3 and axis == 0:
        return tuple(range(bricks))
    reach = {1: 1, 2: 3, 3: 5}[level]
    return tuple(range(-reach, reach + 1))


def weight_sections(count_x, count_y):
    sections, start = {}, 0
    for level in (1, 2, 3):
        for axis, bricks in ((0, count_x), (1, count_y)):
            offsets = brick_offsets(level, axis, bricks)
            sections[level, axis] = (start, offsets)
            start += len(offsets)
    return sections, start


def split(values):
    high = values.astype(jnp.bfloat16)
    return high, (values - high.astype(jnp.float32)).astype(jnp.bfloat16)


def dot(left, right):
    return lax.dot_general(left, right, (((1,), (0,)), ((), ())), preferred_element_type=jnp.float32)


def dot_lanes(left, right):
    return lax.dot_general(left, right, (((1,), (1,)), ((), ())), preferred_element_type=jnp.float32)


def wrapped(values, margin, axis):
    size = values.shape[axis]
    tail = lax.slice_in_dim(values, size - margin, size, axis=axis)
    head = lax.slice_in_dim(values, 0, margin, axis=axis)
    return jnp.concatenate([tail, values, head], axis=axis)


def both_ways(product):
    half = product.shape[1] // 2
    return product[:, :half] + product[:, half:]


def side_by_side(values):
    return jnp.concatenate(split(values), axis=1)


def restrict_kernel(
    taps_far, charges_far, constants_far, blocks_far, head, tail, taps, charges, constants, patch, rim, blocks, arrived
):
    rows_x, rows_y, depth = charges.shape
    columns = rows_x * rows_y
    copies = [
        pltpu.make_async_copy(constants_far, constants, arrived.at[0]),
        pltpu.make_async_copy(taps_far, taps, arrived.at[1]),
    ]
    leaving = [
        pltpu.make_async_copy(charges.at[pl.ds(0, 4)], head, arrived.at[2]),
        pltpu.make_async_copy(charges.at[pl.ds(rows_x - 4, 4)], tail, arrived.at[3]),
    ]
    chunks = []
    for index in range(depth // 256):
        section = pl.ds(256 * index, 256)
        chunks.append(
            pltpu.make_async_copy(
                charges_far.at[:, :, section], charges.at[:, :, section], arrived.at[4 + index]
            )
        )
    copies[0].start()
    for chunk in chunks:
        chunk.start()
    copies[1].start()
    copies[0].wait()
    for index, chunk in enumerate(chunks):
        chunk.wait()
        high, low = split(charges[:, :, 256 * index : 256 * (index + 1)].reshape(columns, 256))
        down = constants[:, 0:columns]
        high, low = split(dot(down, high) + dot(down, low))
        begin = lanes + 256 * index
        patch[0:lanes, begin : begin + 256] = high
        patch[lanes : 2 * lanes, begin : begin + 256] = low
    for copy in leaving:
        copy.start()
    patch[:, 0:lanes] = patch[:, depth : depth + lanes]
    patch[:, depth + lanes : depth + 2 * lanes] = patch[:, lanes : 2 * lanes]
    lane_window = constants[:, 256:768]
    row_window = constants[:, 768:1152]
    grid = jnp.concatenate(
        [
            both_ways(dot_lanes(lane_window, patch[:, begin : begin + 512]))
            for begin in range(0, depth, 256)
        ],
        axis=0,
    )
    grids = {1: grid}
    for level in (1, 2):
        cells = grid.shape[0]
        down = constants[:, 1024 + 128 * level : 1152 + 128 * level]
        grid = dot(side_by_side(grid), jnp.concatenate([down, down], axis=0))
        ready = wrapped(side_by_side(grid), 64, 0)
        grid = jnp.concatenate(
            [both_ways(dot(row_window, ready[begin : begin + 384])) for begin in range(0, cells, 256)], axis=0
        )
        grids[level + 1] = grid
    copies[1].wait()
    first = 0
    for level in (1, 2, 3):
        grid = grids[level]
        cells = grid.shape[0]
        rim[first : first + 8, :] = grid[cells - 8 :, :]
        rim[first + 8 : first + 8 + cells, :] = grid
        rim[first + 8 + cells : first + 16 + cells, :] = grid[:8, :]
        for index, row in enumerate(block_rows[level]):
            summed = None
            for tap in range(9):
                begin = first + lanes * index + 4 + tap
                term = taps[2, level, tap] * rim[begin : begin + lanes, :]
                summed = term if summed is None else summed + term
            blocks[pl.ds(row, lanes, stride=rows_per_block), :] = summed
        first += cells + 16
    for index in range(4):
        section = pl.ds(224 * index, 224)
        leaving.append(
            pltpu.make_async_copy(blocks.at[section], blocks_far.at[section], arrived.at[4 + depth // 256 + index])
        )
        leaving[-1].start()
    for copy in leaving:
        copy.wait()


def weight_kernel(sections, taps, tables, weights):
    for (level, axis), (start, offsets) in sections.items():
        begin = (2 * (level - 1) + axis) * (2 * lanes + 16)
        chooser = tables[begin : begin + lanes, 0:16]
        same = tables[begin + lanes : begin + 2 * lanes, :]
        base = tables[begin + 2 * lanes : begin + 2 * lanes + 16, :].astype(jnp.float32).astype(jnp.int32)
        scale = 0.5**level if axis == 0 else 1.0
        values = [scale * taps[axis, level, tap] for tap in range(9)]
        for index, offset in enumerate(offsets):
            number = base + brick_cells[level] * offset
            if level == 3 and axis == 0:
                number = number & 271
            chosen = jnp.zeros(number.shape, jnp.float32)
            for tap in range(9):
                chosen = jnp.where(number == tap, values[tap], chosen)
            spread = dot(chooser, side_by_side(chosen)).astype(jnp.bfloat16)
            rows = pl.ds((start + index) * lanes, lanes)
            weights[rows, 0:lanes] = spread[:, :lanes] * same
            weights[rows, lanes : 2 * lanes] = spread[:, lanes:] * same


def weighted(pieces, weights, start):
    rows = pl.ds(start * lanes, len(pieces) * lanes)
    product = both_ways(dot(jnp.concatenate(pieces, axis=1), weights[rows, :]))
    half = product.shape[0] // 2
    return product[:half] + product[half:]


def convolve_kernel(sections, count_x, count_y, received, weights, blocks_far, blocks, left):
    columns = {}
    for level in (1, 2, 3):
        slices = len(block_rows[level])
        values = jnp.concatenate(
            [received[pl.ds(row, lanes, stride=rows_per_block), :] for row in block_rows[level]], axis=0
        )
        start, offsets = sections[level, 0]
        stack = jnp.concatenate(split(values), axis=0).reshape(2 * slices, count_x, count_y, lanes)
        pieces = []
        for offset in offsets:
            turn = offset % count_x
            turned = jnp.concatenate([stack[:, turn:], stack[:, :turn]], axis=1) if turn else stack
            pieces.append(turned.reshape(2 * slices * lanes, lanes))
        columns[level] = weighted(pieces, weights, start)
    for level in (1, 2, 3):
        slices = len(block_rows[level])
        start, offsets = sections[level, 1]
        stack = columns[level].reshape(slices * count_x, count_y, lanes)
        pieces = []
        for offset in offsets:
            turn = offset % count_y
            turned = jnp.concatenate([stack[:, turn:], stack[:, :turn]], axis=1) if turn else stack
            pieces.append(jnp.concatenate(split(turned.reshape(slices * lanes, lanes)), axis=0))
        values = weighted(pieces, weights, start)
        for index, row in enumerate(block_rows[level]):
            blocks[pl.ds(row, lanes, stride=rows_per_block), :] = values[lanes * index : lanes * (index + 1)]
    copies = []
    for index in range(4):
        section = pl.ds(224 * index, 224)
        copies.append(pltpu.make_async_copy(blocks.at[section], blocks_far.at[section], left.at[index]))
        copies[-1].start()
    for copy in copies:
        copy.wait()


def finish_kernel(received, constants, twice_up, finest, potential, ready, left):
    rows_x, rows_y, depth = finest.shape
    row_window = constants[:, 512:768]
    parts = {
        level: jnp.concatenate(
            [received[pl.ds(row, lanes, stride=rows_per_block), :] for row in block_rows[level]], axis=0
        )
        for level in (1, 2, 3)
    }
    high, low = split(parts[3])
    coarsest = dot(jnp.concatenate([high, low, high], axis=1), twice_up[0 : 3 * lanes, :])
    middle = dot(side_by_side(parts[2]), constants[:, 128:256])
    coarsest = both_ways(dot(twice_up[3 * lanes :, :], side_by_side(coarsest)))
    pairs = wrapped(side_by_side(middle), 64, 0)
    middle = jnp.concatenate(
        [
            both_ways(dot(row_window, pairs[begin : begin + 256]))
            for begin in range(0, 2 * lanes, lanes)
        ],
        axis=0,
    )
    running = parts[1] + middle + coarsest
    pairs = wrapped(side_by_side(running), 64, 0)
    copies = []
    for index in range(depth // 256):
        fine = both_ways(dot(row_window, pairs[lanes * index : lanes * index + 256]))
        smooth = dot_lanes(constants[:, 256:512], side_by_side(fine))
        section = slice(256 * index, 256 * (index + 1))
        ready[:, :, section] = finest[:, :, section] + smooth.reshape(rows_x, rows_y, 256)
        places = pl.ds(256 * index, 256)
        copies.append(
            pltpu.make_async_copy(ready.at[:, :, places], potential.at[:, :, places], left.at[index])
        )
        copies[-1].start()
    for copy in copies:
        copy.wait()


def convolve_x_kernel(taps, before, own, after, summed_ref, head, tail):
    rows_x, rows_y, depth = own.shape

    def layer(index):
        if index < 4:
            return before[index]
        return own[index - 4] if index < 4 + rows_x else after[index - 4 - rows_x]

    for row in range(rows_x):
        summed = taps[0, 0, 0] * layer(row)
        for tap in range(1, 9):
            summed = summed + taps[0, 0, tap] * layer(row + tap)
        summed_ref[row] = summed
        head[row] = summed[:4]
        tail[row] = summed[rows_y - 4 :]


def convolve_yz_kernel(taps, before, own, after, result, rim):
    rows_x, rows_y, depth = own.shape
    for row in range(rows_x):
        rim[row, 4:8, :] = before[row]
        rim[row, 8 : 8 + rows_y, :] = own[row]
        rim[row, 8 + rows_y : 12 + rows_y, :] = after[row]
    for row in range(rows_x):
        summed = taps[1, 0, 0] * rim[row, 4 : 4 + rows_y, :]
        for tap in range(1, 9):
            summed = summed + taps[1, 0, tap] * rim[row, 4 + tap : 4 + tap + rows_y, :]
        total = taps[2, 0, 4] * summed
        for tap in (0, 1, 2, 3, 5, 6, 7, 8):
            total = total + taps[2, 0, tap] * pltpu.roll(summed, (4 - tap) % depth, 1)
        result[row] = total


def in_vmem(count):
    return [pl.BlockSpec(memory_space=pltpu.VMEM)] * count


scalars = pl.BlockSpec(memory_space=pltpu.SMEM)
far = pl.BlockSpec(memory_space=pltpu.HBM)


def shape_of(*shape, dtype=jnp.float32):
    return jax.ShapeDtypeStruct(shape, dtype)


def call(kernel, outs, in_specs, scratch=(), out_specs=None, limit=16, flops=0, moved=0):
    if out_specs is None:
        out_specs = jax.tree.map(lambda _: pl.BlockSpec(memory_space=pltpu.VMEM), outs)
    return pl.pallas_call(
        kernel,
        out_shape=outs,
        in_specs=in_specs,
        out_specs=out_specs,
        scratch_shapes=list(scratch),
        compiler_params=pltpu.CompilerParams(vmem_limit_bytes=limit * 2**20),
        cost_estimate=pl.CostEstimate(flops=flops, bytes_accessed=moved, transcendentals=0),
    )


def per_device(charges, kernel_taps):
    count_x, count_y = lax.axis_size("gx"), lax.axis_size("gy")
    rows_x, rows_y, depth = charges.shape
    taps = jnp.transpose(kernel_taps, (1, 0, 2))
    both = ("gx", "gy")
    downs = [restrict_1d(level) for level in range(3)]
    ups = [prolong_1d(level) for level in range(3)]
    down_constants = np.concatenate(
        [
            padded(np.kron(downs[0], downs[0]), lanes, rows_x * rows_y),
            restrict_window(lanes, 512, 128),
            restrict_window(lanes, 384, 64),
            padded(np.kron(downs[1].T, downs[1].T), lanes, lanes),
            padded(np.kron(downs[2].T, downs[2].T), lanes, lanes),
        ],
        axis=1,
    )
    down_constants = jnp.asarray(down_constants, jnp.bfloat16)

    def twice(matrix, axis):
        return np.concatenate([matrix, matrix], axis=axis)

    up_1, up_2, up_3 = (
        padded(matrix, rows, lanes)
        for matrix, rows in (
            (np.kron(ups[0], ups[0]), 256),
            (np.kron(ups[1].T, ups[1].T), lanes),
            (np.kron(ups[2].T, ups[2].T), lanes),
        )
    )
    up_constants = jnp.asarray(
        np.concatenate(
            [twice(up_3, 0), twice(up_2, 0), twice(up_1, 1), prolong_window(256, 256, 64)], axis=1
        ),
        jnp.bfloat16,
    )
    both_ups = padded(np.kron((ups[1] @ ups[2]).T, (ups[1] @ ups[2]).T), lanes, lanes)
    rounded = both_ups.astype(jnp.bfloat16).astype(np.float32)
    twice_up = jnp.asarray(
        np.concatenate(
            [rounded, rounded, both_ups - rounded, prolong_ring(4 * lanes) @ prolong_ring(2 * lanes)], axis=0
        ),
        jnp.bfloat16,
    )
    sections, section_count = weight_sections(count_x, count_y)
    block_shape = (lanes * rows_per_block, lanes)
    exchange_shape = (lanes * rows_per_block, 1, lanes)

    blocks, head, tail = call(
        restrict_kernel,
        (
            shape_of(*block_shape),
            shape_of(4, rows_y, depth),
            shape_of(4, rows_y, depth),
        ),
        [far] * 3,
        [
            pltpu.SMEM(taps.shape, jnp.float32),
            pltpu.VMEM((rows_x, rows_y, depth), jnp.float32),
            pltpu.VMEM(down_constants.shape, jnp.bfloat16),
            pltpu.VMEM((2 * lanes, depth + 2 * lanes), jnp.bfloat16),
            pltpu.VMEM((7 * lanes + 48, lanes), jnp.float32),
            pltpu.VMEM(block_shape, jnp.float32),
            pltpu.SemaphoreType.DMA((8 + depth // 256,)),
        ],
        (far,) * 3,
        limit=60,
        flops=10**9,
        moved=2 * 10**6,
    )(taps, charges, down_constants)
    received = lax.all_to_all(blocks.reshape(exchange_shape), both, 0, 0, tiled=True)

    weights = call(
        lambda *refs: weight_kernel(sections, *refs),
        shape_of(section_count * lanes, 2 * lanes, dtype=jnp.bfloat16),
        [scalars] + in_vmem(1),
        flops=2 * 10**7,
        moved=3 * 10**6,
    )(taps, tap_tables())

    def shifted(values, axis, step):
        count = lax.axis_size(axis)
        return lax.ppermute(values, axis, [(i, (i + step) % count) for i in range(count)])

    before = shifted(tail, "gx", 1)
    after = shifted(head, "gx", -1)
    summed, head, tail = call(
        convolve_x_kernel,
        (shape_of(rows_x, rows_y, depth), shape_of(rows_x, 4, depth), shape_of(rows_x, 4, depth)),
        [scalars] + in_vmem(3),
        flops=10**11,
        moved=3 * 10**6,
    )(taps, before, charges, after)
    received, _ = lax.optimization_barrier((received, tail))
    finest = call(
        convolve_yz_kernel,
        shape_of(rows_x, rows_y, depth),
        [scalars] + in_vmem(3),
        [pltpu.VMEM((rows_x, rows_y + 16, depth), jnp.float32)],
        flops=10**11,
        moved=3 * 10**6,
    )(taps, shifted(tail, "gy", 1), summed, shifted(head, "gy", -1))

    blocks = call(
        lambda *refs: convolve_kernel(sections, count_x, count_y, *refs),
        shape_of(*block_shape),
        in_vmem(2),
        [pltpu.VMEM(block_shape, jnp.float32), pltpu.SemaphoreType.DMA((4,))],
        far,
        flops=10**9,
        moved=4 * 10**6,
    )(received.reshape(block_shape), weights)
    received = lax.all_to_all(blocks.reshape(exchange_shape), both, 0, 0, tiled=True)

    return call(
        finish_kernel,
        shape_of(rows_x, rows_y, depth),
        in_vmem(4),
        [pltpu.VMEM((rows_x, rows_y, depth), jnp.float32), pltpu.SemaphoreType.DMA((depth // 256,))],
        far,
        flops=10**9,
        moved=4 * 10**6,
    )(received.reshape(block_shape), up_constants, twice_up, finest)


def solution(mesh):
    placed = (P("gx", "gy", None), P())
    return jax.shard_map(
        per_device, mesh=mesh, in_specs=placed, out_specs=P("gx", "gy", None), check_vma=False
    )
```

```python
import jax
import jax.numpy as jnp
import numpy as np
from jax import lax
from jax.experimental import pallas as pl
from jax.experimental.pallas import tpu as pltpu
from jax.sharding import PartitionSpec as P

first_cell = (0, -1, -2, -2)
cell_count = (16, 11, 9, 7)
brick_cells = (16, 8, 4, 2)
restrict_taps = {-3: -0.0625, -1: 0.5625, 0: 1.0, 1: 0.5625, 3: -0.0625}
lanes = 128
block_rows = ((), (0, 1, 2, 3), (4, 5), (6,))
rows_per_block = 7


def restrict_1d(level):
    matrix = np.zeros((cell_count[level + 1], cell_count[level]), np.float32)
    for coarse in range(cell_count[level + 1]):
        for fine in range(cell_count[level]):
            offset = first_cell[level] + fine - 2 * (first_cell[level + 1] + coarse)
            matrix[coarse, fine] = restrict_taps.get(offset, 0.0)
    return matrix


def prolong_entries(fine):
    if fine % 2 == 0:
        return {fine // 2: 1.0}
    left = (fine - 1) // 2
    return {left - 1: -0.0625, left: 0.5625, left + 1: 0.5625, left + 2: -0.0625}


def prolong_1d(level):
    matrix = np.zeros((cell_count[level], cell_count[level + 1]), np.float32)
    for fine in range(cell_count[level]):
        for coarse, weight in prolong_entries(first_cell[level] + fine).items():
            matrix[fine, coarse - first_cell[level + 1]] = weight
    return matrix


def padded(matrix, rows, columns):
    result = np.zeros((rows, columns), np.float32)
    result[: matrix.shape[0], : matrix.shape[1]] = matrix
    return result


def restrict_window(rows, width, margin):
    matrix = np.zeros((rows, width), np.float32)
    for coarse in range(rows):
        for offset, weight in restrict_taps.items():
            matrix[coarse, margin + 2 * coarse + offset] = weight
    return matrix


def prolong_window(rows, width, margin):
    matrix = np.zeros((rows, width), np.float32)
    for fine in range(rows):
        for coarse, weight in prolong_entries(fine).items():
            matrix[fine, margin + coarse] = weight
    return matrix


def prolong_ring(rows):
    matrix = np.zeros((rows, rows // 2), np.float32)
    for fine in range(rows):
        for coarse, weight in prolong_entries(fine).items():
            matrix[fine, coarse % (rows // 2)] = weight
    return matrix


def to_level(level):
    down = up = np.eye(cell_count[1], dtype=np.float32)
    for step in range(1, level):
        down, up = restrict_1d(step) @ down, up @ prolong_1d(step)
    return down, up


def tap_tables():
    count = cell_count[1]
    cells = [divmod(cell, count) for cell in range(count * count)]
    tables = []
    for axis in (0, 1):
        same = np.zeros((lanes, lanes), np.float32)
        for row, here in enumerate(cells):
            for column, there in enumerate(cells):
                same[row, column] = here[1 - axis] == there[1 - axis]
        tables.append(same)
    for level in (1, 2, 3):
        down, up = to_level(level)
        size = cell_count[level]
        for axis in (0, 1):
            into, out_of = np.zeros((lanes, lanes), np.float32), np.zeros((16, lanes), np.float32)
            number = np.full((16, lanes), 256.0, np.float32)
            for cell, place in enumerate(cells):
                into[cell, :size] = down[:, place[axis]]
                out_of[:size, cell] = up[place[axis], :]
            for source in range(size):
                for wanted in range(size):
                    number[source, wanted] = source - wanted + 4
            tables += [into, out_of, number]
    return jnp.asarray(np.concatenate(tables), jnp.bfloat16)


def brick_offsets(level, axis, bricks):
    if level == 3 and axis == 0:
        return tuple(range(bricks))
    reach = {1: 1, 2: 3, 3: 5}[level]
    return tuple(range(-reach, reach + 1))


def weight_sections(count_x, count_y):
    sections, start = {}, 0
    for level in (1, 2, 3):
        for axis, bricks in ((0, count_x), (1, count_y)):
            offsets = brick_offsets(level, axis, bricks)
            sections[level, axis] = (start, offsets)
            start += len(offsets)
    return sections, start


def split(values):
    high = values.astype(jnp.bfloat16)
    return high, (values - high.astype(jnp.float32)).astype(jnp.bfloat16)


def dot(left, right):
    return lax.dot_general(left, right, (((1,), (0,)), ((), ())), preferred_element_type=jnp.float32)


def dot_lanes(left, right):
    return lax.dot_general(left, right, (((1,), (1,)), ((), ())), preferred_element_type=jnp.float32)


def wrapped(values, margin, axis):
    size = values.shape[axis]
    tail = lax.slice_in_dim(values, size - margin, size, axis=axis)
    head = lax.slice_in_dim(values, 0, margin, axis=axis)
    return jnp.concatenate([tail, values, head], axis=axis)


def both_ways(product):
    half = product.shape[1] // 2
    return product[:, :half] + product[:, half:]


def side_by_side(values):
    return jnp.concatenate(split(values), axis=1)


def restrict_kernel(
    taps_far, charges_far, constants_far, blocks_far, head, tail, taps, charges, constants, patch, rim, blocks, arrived
):
    rows_x, rows_y, depth = charges.shape
    columns = rows_x * rows_y
    copies = [
        pltpu.make_async_copy(constants_far, constants, arrived.at[0]),
        pltpu.make_async_copy(taps_far, taps, arrived.at[1]),
    ]
    leaving = [
        pltpu.make_async_copy(charges.at[:, pl.ds(0, 4)], head, arrived.at[2]),
        pltpu.make_async_copy(charges.at[:, pl.ds(rows_y - 4, 4)], tail, arrived.at[3]),
    ]
    chunks = []
    for index in range(depth // 256):
        section = pl.ds(256 * index, 256)
        chunks.append(
            pltpu.make_async_copy(
                charges_far.at[:, :, section], charges.at[:, :, section], arrived.at[4 + index]
            )
        )
    copies[0].start()
    for chunk in chunks:
        chunk.start()
    copies[1].start()
    copies[0].wait()
    for index, chunk in enumerate(chunks):
        chunk.wait()
        high, low = split(charges[:, :, 256 * index : 256 * (index + 1)].reshape(columns, 256))
        down = constants[:, 0:columns]
        high, low = split(dot(down, high) + dot(down, low))
        begin = lanes + 256 * index
        patch[0:lanes, begin : begin + 256] = high
        patch[lanes : 2 * lanes, begin : begin + 256] = low
    for copy in leaving:
        copy.start()
    patch[:, 0:lanes] = patch[:, depth : depth + lanes]
    patch[:, depth + lanes : depth + 2 * lanes] = patch[:, lanes : 2 * lanes]
    lane_window = constants[:, 256:768]
    row_window = constants[:, 768:1152]
    grid = jnp.concatenate(
        [
            both_ways(dot_lanes(lane_window, patch[:, begin : begin + 512]))
            for begin in range(0, depth, 256)
        ],
        axis=0,
    )
    grids = {1: grid}
    for level in (1, 2):
        ready = wrapped(side_by_side(grid), 64, 0)
        grid = jnp.concatenate(
            [
                both_ways(dot(row_window, ready[begin : begin + 384]))
                for begin in range(0, grid.shape[0], 256)
            ],
            axis=0,
        )
        grids[level + 1] = grid
    copies[1].wait()
    first = 0
    for level in (1, 2, 3):
        grid = grids[level]
        cells = grid.shape[0]
        rim[first : first + 8, :] = grid[cells - 8 :, :]
        rim[first + 8 : first + 8 + cells, :] = grid
        rim[first + 8 + cells : first + 16 + cells, :] = grid[:8, :]
        for index, row in enumerate(block_rows[level]):
            summed = None
            for tap in range(9):
                begin = first + lanes * index + 4 + tap
                term = taps[2, level, tap] * rim[begin : begin + lanes, :]
                summed = term if summed is None else summed + term
            blocks[pl.ds(row, lanes, stride=rows_per_block), :] = summed
        first += cells + 16
    for index in range(4):
        section = pl.ds(224 * index, 224)
        leaving.append(
            pltpu.make_async_copy(blocks.at[section], blocks_far.at[section], arrived.at[4 + depth // 256 + index])
        )
        leaving[-1].start()
    for copy in leaving:
        copy.wait()


def weight_kernel(sections, taps, tables, weights):
    tables_at = {
        (level, axis): 2 * lanes + (2 * (level - 1) + axis) * (lanes + 32) for level, axis in sections
    }
    stacks = {}
    for (level, axis), (start, offsets) in sections.items():
        begin = tables_at[level, axis] + lanes + 16
        base = tables[begin : begin + 16, :].astype(jnp.float32).astype(jnp.int32)
        scale = 0.5**level if axis == 0 else 1.0
        values = [scale * taps[axis, level, tap] for tap in range(9)]
        stack = []
        for offset in offsets:
            number = base + brick_cells[level] * offset
            if level == 3 and axis == 0:
                number = number & 271
            chosen = jnp.zeros(number.shape, jnp.float32)
            for tap in range(9):
                chosen = jnp.where(number == tap, values[tap], chosen)
            stack.append(chosen)
        stacks[level, axis] = split(jnp.concatenate(stack, axis=0))
    for level, axis in sections:
        begin = tables_at[level, axis] + lanes
        high, low = stacks[level, axis]
        out_of = tables[begin : begin + 16, :]
        stacks[level, axis] = split(dot(high[:, 0:16], out_of) + dot(low[:, 0:16], out_of))
    for (level, axis), (start, offsets) in sections.items():
        same = tables[axis * lanes : (axis + 1) * lanes, :].astype(jnp.float32)
        into = tables[tables_at[level, axis] : tables_at[level, axis] + lanes, 0:16]
        into = jnp.concatenate([into, into], axis=1)
        for index in range(0, len(offsets), 2):
            pair = range(index, min(index + 2, len(offsets)))
            parts = [
                jnp.concatenate([half[16 * part : 16 * (part + 1)] for part in pair], axis=1)
                for half in stacks[level, axis]
            ]
            spread = dot(into, jnp.concatenate(parts, axis=0))
            for place, part in enumerate(pair):
                rows = pl.ds((start + part) * lanes, lanes)
                weights[rows, :] = side_by_side(spread[:, place * lanes : (place + 1) * lanes] * same)


def weighted(pieces, weights, start):
    rows = pl.ds(start * lanes, len(pieces) * lanes)
    product = both_ways(dot(jnp.concatenate(pieces, axis=1), weights[rows, :]))
    half = product.shape[0] // 2
    return product[:half] + product[half:]


def convolve_kernel(sections, count_x, count_y, received, weights, blocks_far, blocks, left):
    columns = {}
    for level in (1, 2, 3):
        slices = len(block_rows[level])
        values = jnp.concatenate(
            [received[pl.ds(row, lanes, stride=rows_per_block), :] for row in block_rows[level]], axis=0
        )
        start, offsets = sections[level, 0]
        stack = jnp.concatenate(split(values), axis=0).reshape(2 * slices, count_x, count_y, lanes)
        pieces = []
        for offset in offsets:
            turn = offset % count_x
            turned = jnp.concatenate([stack[:, turn:], stack[:, :turn]], axis=1) if turn else stack
            pieces.append(turned.reshape(2 * slices * lanes, lanes))
        columns[level] = weighted(pieces, weights, start)
    for level in (1, 2, 3):
        slices = len(block_rows[level])
        start, offsets = sections[level, 1]
        stack = columns[level].reshape(slices * count_x, count_y, lanes)
        pieces = []
        for offset in offsets:
            turn = offset % count_y
            turned = jnp.concatenate([stack[:, turn:], stack[:, :turn]], axis=1) if turn else stack
            pieces.append(jnp.concatenate(split(turned.reshape(slices * lanes, lanes)), axis=0))
        values = weighted(pieces, weights, start)
        for index, row in enumerate(block_rows[level]):
            blocks[pl.ds(row, lanes, stride=rows_per_block), :] = values[lanes * index : lanes * (index + 1)]
    copies = []
    for index in range(4):
        section = pl.ds(224 * index, 224)
        copies.append(pltpu.make_async_copy(blocks.at[section], blocks_far.at[section], left.at[index]))
        copies[-1].start()
    for copy in copies:
        copy.wait()


def finish_kernel(received, constants, twice_up, finest, potential, ready, left):
    rows_x, rows_y, depth = finest.shape
    row_window = constants[:, 256:512]
    parts = {
        level: jnp.concatenate(
            [received[pl.ds(row, lanes, stride=rows_per_block), :] for row in block_rows[level]], axis=0
        )
        for level in (1, 2, 3)
    }
    coarsest = both_ways(dot(twice_up[...], side_by_side(parts[3])))
    pairs = wrapped(side_by_side(parts[2]), 64, 0)
    middle = jnp.concatenate(
        [both_ways(dot(row_window, pairs[begin : begin + 256])) for begin in (0, lanes)], axis=0
    )
    running = parts[1] + middle + coarsest
    pairs = wrapped(side_by_side(running), 64, 0)
    copies = []
    for index in range(depth // 256):
        fine = both_ways(dot(row_window, pairs[lanes * index : lanes * index + 256]))
        smooth = dot_lanes(constants[:, 0:256], side_by_side(fine))
        section = slice(256 * index, 256 * (index + 1))
        ready[:, :, section] = finest[:, :, section] + smooth.reshape(rows_x, rows_y, 256)
        places = pl.ds(256 * index, 256)
        copies.append(
            pltpu.make_async_copy(ready.at[:, :, places], potential.at[:, :, places], left.at[index])
        )
        copies[-1].start()
    for copy in copies:
        copy.wait()


def convolve_y_kernel(taps, before, own, after, summed_ref, head, tail):
    rows_x, rows_y, depth = own.shape
    for row in range(rows_x):
        lines = jnp.concatenate([before[row], own[row], after[row]], axis=0)
        summed = taps[1, 0, 0] * lines[0:rows_y]
        for tap in range(1, 9):
            summed = summed + taps[1, 0, tap] * lines[tap : tap + rows_y]
        summed_ref[row] = summed
        if row < 4:
            head[row] = summed
        if row >= rows_x - 4:
            tail[row - (rows_x - 4)] = summed


def convolve_xz_kernel(taps, before, own, after, result):
    rows_x, rows_y, depth = own.shape

    def layer(index):
        if index < 4:
            return before[index]
        return own[index - 4] if index < 4 + rows_x else after[index - 4 - rows_x]

    for row in range(rows_x):
        summed = taps[0, 0, 0] * layer(row)
        for tap in range(1, 9):
            summed = summed + taps[0, 0, tap] * layer(row + tap)
        total = taps[2, 0, 4] * summed
        for tap in (0, 1, 2, 3, 5, 6, 7, 8):
            total = total + taps[2, 0, tap] * pltpu.roll(summed, (4 - tap) % depth, 1)
        result[row] = total


def in_vmem(count):
    return [pl.BlockSpec(memory_space=pltpu.VMEM)] * count


scalars = pl.BlockSpec(memory_space=pltpu.SMEM)
far = pl.BlockSpec(memory_space=pltpu.HBM)


def shape_of(*shape, dtype=jnp.float32):
    return jax.ShapeDtypeStruct(shape, dtype)


def call(kernel, outs, in_specs, scratch=(), out_specs=None, limit=16, flops=0, moved=0):
    if out_specs is None:
        out_specs = jax.tree.map(lambda _: pl.BlockSpec(memory_space=pltpu.VMEM), outs)
    return pl.pallas_call(
        kernel,
        out_shape=outs,
        in_specs=in_specs,
        out_specs=out_specs,
        scratch_shapes=list(scratch),
        compiler_params=pltpu.CompilerParams(vmem_limit_bytes=limit * 2**20),
        cost_estimate=pl.CostEstimate(flops=flops, bytes_accessed=moved, transcendentals=0),
    )


def per_device(charges, kernel_taps):
    count_x, count_y = lax.axis_size("gx"), lax.axis_size("gy")
    rows_x, rows_y, depth = charges.shape
    taps = jnp.transpose(kernel_taps, (1, 0, 2))
    both = ("gx", "gy")
    down, up = restrict_1d(0), prolong_1d(0)
    down_constants = np.concatenate(
        [
            padded(np.kron(down, down), lanes, rows_x * rows_y),
            restrict_window(lanes, 512, 128),
            restrict_window(lanes, 384, 64),
        ],
        axis=1,
    )
    down_constants = jnp.asarray(down_constants, jnp.bfloat16)

    up_1 = padded(np.kron(up, up), rows_x * rows_y, lanes)
    up_constants = jnp.asarray(
        np.concatenate([up_1, up_1, prolong_window(256, 256, 64)], axis=1), jnp.bfloat16
    )
    twice_up = jnp.asarray(prolong_ring(4 * lanes) @ prolong_ring(2 * lanes), jnp.bfloat16)
    sections, section_count = weight_sections(count_x, count_y)
    block_shape = (lanes * rows_per_block, lanes)
    exchange_shape = (lanes * rows_per_block, 1, lanes)

    blocks, head, tail = call(
        restrict_kernel,
        (
            shape_of(*block_shape),
            shape_of(rows_x, 4, depth),
            shape_of(rows_x, 4, depth),
        ),
        [far] * 3,
        [
            pltpu.SMEM(taps.shape, jnp.float32),
            pltpu.VMEM((rows_x, rows_y, depth), jnp.float32),
            pltpu.VMEM(down_constants.shape, jnp.bfloat16),
            pltpu.VMEM((2 * lanes, depth + 2 * lanes), jnp.bfloat16),
            pltpu.VMEM((7 * lanes + 48, lanes), jnp.float32),
            pltpu.VMEM(block_shape, jnp.float32),
            pltpu.SemaphoreType.DMA((8 + depth // 256,)),
        ],
        (far,) * 3,
        limit=60,
        flops=10**9,
        moved=2 * 10**6,
    )(taps, charges, down_constants)
    received = lax.all_to_all(blocks.reshape(exchange_shape), both, 0, 0, tiled=True)

    weights = call(
        lambda *refs: weight_kernel(sections, *refs),
        shape_of(section_count * lanes, 2 * lanes, dtype=jnp.bfloat16),
        [scalars] + in_vmem(1),
        flops=2 * 10**7,
        moved=3 * 10**6,
    )(taps, tap_tables())

    def shifted(values, axis, step):
        count = lax.axis_size(axis)
        return lax.ppermute(values, axis, [(i, (i + step) % count) for i in range(count)])

    before = shifted(tail, "gy", 1)
    after = shifted(head, "gy", -1)
    summed, head, tail = call(
        convolve_y_kernel,
        (shape_of(rows_x, rows_y, depth), shape_of(4, rows_y, depth), shape_of(4, rows_y, depth)),
        [scalars] + in_vmem(3),
        flops=10**11,
        moved=3 * 10**6,
    )(taps, before, charges, after)
    received, _ = lax.optimization_barrier((received, tail))
    finest = call(
        convolve_xz_kernel,
        shape_of(rows_x, rows_y, depth),
        [scalars] + in_vmem(3),
        flops=10**11,
        moved=3 * 10**6,
    )(taps, shifted(tail, "gx", 1), summed, shifted(head, "gx", -1))

    blocks = call(
        lambda *refs: convolve_kernel(sections, count_x, count_y, *refs),
        shape_of(*block_shape),
        in_vmem(2),
        [pltpu.VMEM(block_shape, jnp.float32), pltpu.SemaphoreType.DMA((4,))],
        far,
        flops=10**9,
        moved=4 * 10**6,
    )(received.reshape(block_shape), weights)
    received = lax.all_to_all(blocks.reshape(exchange_shape), both, 0, 0, tiled=True)

    return call(
        finish_kernel,
        shape_of(rows_x, rows_y, depth),
        in_vmem(4),
        [pltpu.VMEM((rows_x, rows_y, depth), jnp.float32), pltpu.SemaphoreType.DMA((depth // 256,))],
        far,
        flops=10**9,
        moved=4 * 10**6,
    )(received.reshape(block_shape), up_constants, twice_up, finest)


def solution(mesh):
    placed = (P("gx", "gy", None), P())
    return jax.shard_map(
        per_device, mesh=mesh, in_specs=placed, out_specs=P("gx", "gy", None), check_vma=False
    )
```

```python
import jax
import jax.numpy as jnp
import numpy as np
from jax import lax
from jax.experimental import pallas as pl
from jax.experimental.pallas import tpu as pltpu
from jax.sharding import PartitionSpec as P

first_cell = (0, -1, -2, -2)
cell_count = (16, 11, 9, 7)
brick_cells = (16, 8, 4, 2)
restrict_taps = {-3: -0.0625, -1: 0.5625, 0: 1.0, 1: 0.5625, 3: -0.0625}
lanes = 128
block_rows = ((), (0, 1, 2, 3), (4, 5), (6,))
rows_per_block = 7


def restrict_1d(level):
    matrix = np.zeros((cell_count[level + 1], cell_count[level]), np.float32)
    for coarse in range(cell_count[level + 1]):
        for fine in range(cell_count[level]):
            offset = first_cell[level] + fine - 2 * (first_cell[level + 1] + coarse)
            matrix[coarse, fine] = restrict_taps.get(offset, 0.0)
    return matrix


def prolong_entries(fine):
    if fine % 2 == 0:
        return {fine // 2: 1.0}
    left = (fine - 1) // 2
    return {left - 1: -0.0625, left: 0.5625, left + 1: 0.5625, left + 2: -0.0625}


def prolong_1d(level):
    matrix = np.zeros((cell_count[level], cell_count[level + 1]), np.float32)
    for fine in range(cell_count[level]):
        for coarse, weight in prolong_entries(first_cell[level] + fine).items():
            matrix[fine, coarse - first_cell[level + 1]] = weight
    return matrix


def padded(matrix, rows, columns):
    result = np.zeros((rows, columns), np.float32)
    result[: matrix.shape[0], : matrix.shape[1]] = matrix
    return result


def restrict_window(rows, width, margin):
    matrix = np.zeros((rows, width), np.float32)
    for coarse in range(rows):
        for offset, weight in restrict_taps.items():
            matrix[coarse, margin + 2 * coarse + offset] = weight
    return matrix


def prolong_window(rows, width, margin):
    matrix = np.zeros((rows, width), np.float32)
    for fine in range(rows):
        for coarse, weight in prolong_entries(fine).items():
            matrix[fine, margin + coarse] = weight
    return matrix


def prolong_ring(rows):
    matrix = np.zeros((rows, rows // 2), np.float32)
    for fine in range(rows):
        for coarse, weight in prolong_entries(fine).items():
            matrix[fine, coarse % (rows // 2)] = weight
    return matrix


def to_level(level):
    down = up = np.eye(cell_count[1], dtype=np.float32)
    for step in range(1, level):
        down, up = restrict_1d(step) @ down, up @ prolong_1d(step)
    return down, up


def tap_tables():
    count = cell_count[1]
    cells = [divmod(cell, count) for cell in range(count * count)]
    tables = []
    for axis in (0, 1):
        same = np.zeros((lanes, lanes), np.float32)
        for row, here in enumerate(cells):
            for column, there in enumerate(cells):
                same[row, column] = here[1 - axis] == there[1 - axis]
        tables.append(same)
    for level in (1, 2, 3):
        down, up = to_level(level)
        size = cell_count[level]
        for axis in (0, 1):
            into, out_of = np.zeros((lanes, lanes), np.float32), np.zeros((16, lanes), np.float32)
            number = np.full((16, lanes), 256.0, np.float32)
            for cell, place in enumerate(cells):
                into[cell, :size] = down[:, place[axis]]
                out_of[:size, cell] = up[place[axis], :]
            for source in range(size):
                for wanted in range(size):
                    number[source, wanted] = source - wanted + 4
            tables += [into, out_of, number]
    return jnp.asarray(np.concatenate(tables), jnp.bfloat16)


def brick_offsets(level, axis, bricks):
    if level == 3 and axis == 0:
        return tuple(range(bricks))
    reach = {1: 1, 2: 3, 3: 5}[level]
    return tuple(range(-reach, reach + 1))


def weight_sections(count_x, count_y):
    sections, start = {}, 0
    for level in (1, 2, 3):
        for axis, bricks in ((0, count_x), (1, count_y)):
            offsets = brick_offsets(level, axis, bricks)
            sections[level, axis] = (start, offsets)
            start += len(offsets)
    return sections, start


def split(values):
    high = values.astype(jnp.bfloat16)
    return high, (values - high.astype(jnp.float32)).astype(jnp.bfloat16)


def dot(left, right):
    return lax.dot_general(left, right, (((1,), (0,)), ((), ())), preferred_element_type=jnp.float32)


def dot_lanes(left, right):
    return lax.dot_general(left, right, (((1,), (1,)), ((), ())), preferred_element_type=jnp.float32)


def wrapped(values, margin, axis):
    size = values.shape[axis]
    tail = lax.slice_in_dim(values, size - margin, size, axis=axis)
    head = lax.slice_in_dim(values, 0, margin, axis=axis)
    return jnp.concatenate([tail, values, head], axis=axis)


def both_ways(product):
    half = product.shape[1] // 2
    return product[:, :half] + product[:, half:]


def side_by_side(values):
    return jnp.concatenate(split(values), axis=1)


def restrict_kernel(
    taps_far, charges_far, constants_far, blocks_far, head, tail, taps, charges, constants, patch, rim, blocks, arrived
):
    rows_x, rows_y, depth = charges.shape
    columns = rows_x * rows_y
    copies = [
        pltpu.make_async_copy(constants_far, constants, arrived.at[0]),
        pltpu.make_async_copy(taps_far, taps, arrived.at[1]),
    ]
    leaving = [
        pltpu.make_async_copy(charges.at[:, pl.ds(0, 4)], head, arrived.at[2]),
        pltpu.make_async_copy(charges.at[:, pl.ds(rows_y - 4, 4)], tail, arrived.at[3]),
    ]
    chunks = []
    for index in range(depth // 256):
        section = pl.ds(256 * index, 256)
        chunks.append(
            pltpu.make_async_copy(
                charges_far.at[:, :, section], charges.at[:, :, section], arrived.at[4 + index]
            )
        )
    copies[0].start()
    for chunk in chunks:
        chunk.start()
    copies[1].start()
    copies[0].wait()
    for index, chunk in enumerate(chunks):
        chunk.wait()
        high, low = split(charges[:, :, 256 * index : 256 * (index + 1)].reshape(columns, 256))
        down = constants[:, 0:columns]
        high, low = split(dot(down, high) + dot(down, low))
        begin = lanes + 256 * index
        patch[0:lanes, begin : begin + 256] = high
        patch[lanes : 2 * lanes, begin : begin + 256] = low
    for copy in leaving:
        copy.start()
    patch[:, 0:lanes] = patch[:, depth : depth + lanes]
    patch[:, depth + lanes : depth + 2 * lanes] = patch[:, lanes : 2 * lanes]
    lane_window = constants[:, 256:768]
    row_window = constants[:, 768:1152]
    grid = jnp.concatenate(
        [
            both_ways(dot_lanes(lane_window, patch[:, begin : begin + 512]))
            for begin in range(0, depth, 256)
        ],
        axis=0,
    )
    grids = {1: grid}
    for level in (1, 2):
        ready = wrapped(side_by_side(grid), 64, 0)
        grid = jnp.concatenate(
            [
                both_ways(dot(row_window, ready[begin : begin + 384]))
                for begin in range(0, grid.shape[0], 256)
            ],
            axis=0,
        )
        grids[level + 1] = grid
    copies[1].wait()
    firsts, first = {}, 0
    for level in (1, 2, 3):
        grid = grids[level]
        cells = grid.shape[0]
        rim[first : first + 8, :] = grid[cells - 8 :, :]
        rim[first + 8 : first + 8 + cells, :] = grid
        rim[first + 8 + cells : first + 16 + cells, :] = grid[:8, :]
        firsts[level] = first
        first += cells + 16
    share = lanes // 4
    for part in range(4):
        for level in (1, 2, 3):
            for index, row in enumerate(block_rows[level]):
                summed = None
                for tap in range(9):
                    begin = firsts[level] + lanes * index + share * part + 4 + tap
                    term = taps[2, level, tap] * rim[begin : begin + share, :]
                    summed = term if summed is None else summed + term
                blocks[pl.ds(rows_per_block * share * part + row, share, stride=rows_per_block), :] = summed
        section = pl.ds(rows_per_block * share * part, rows_per_block * share)
        leaving.append(
            pltpu.make_async_copy(blocks.at[section], blocks_far.at[section], arrived.at[4 + depth // 256 + part])
        )
        leaving[-1].start()
    for copy in leaving:
        copy.wait()


def weight_kernel(sections, taps, tables, weights):
    tables_at = {
        (level, axis): 2 * lanes + (2 * (level - 1) + axis) * (lanes + 32) for level, axis in sections
    }
    stacks = {}
    for (level, axis), (start, offsets) in sections.items():
        begin = tables_at[level, axis] + lanes + 16
        base = tables[begin : begin + 16, :].astype(jnp.float32).astype(jnp.int32)
        scale = 0.5**level if axis == 0 else 1.0
        values = [scale * taps[axis, level, tap] for tap in range(9)]
        stack = []
        for offset in offsets:
            number = base + brick_cells[level] * offset
            if level == 3 and axis == 0:
                number = number & 271
            chosen = jnp.zeros(number.shape, jnp.float32)
            for tap in range(9):
                chosen = jnp.where(number == tap, values[tap], chosen)
            stack.append(chosen)
        stacks[level, axis] = split(jnp.concatenate(stack, axis=0))
    for level, axis in sections:
        begin = tables_at[level, axis] + lanes
        high, low = stacks[level, axis]
        out_of = tables[begin : begin + 16, :]
        stacks[level, axis] = split(dot(high[:, 0:16], out_of) + dot(low[:, 0:16], out_of))
    for (level, axis), (start, offsets) in sections.items():
        same = tables[axis * lanes : (axis + 1) * lanes, :].astype(jnp.float32)
        into = tables[tables_at[level, axis] : tables_at[level, axis] + lanes, 0:16]
        into = jnp.concatenate([into, into], axis=1)
        for index in range(0, len(offsets), 2):
            pair = range(index, min(index + 2, len(offsets)))
            parts = [
                jnp.concatenate([half[16 * part : 16 * (part + 1)] for part in pair], axis=1)
                for half in stacks[level, axis]
            ]
            spread = dot(into, jnp.concatenate(parts, axis=0))
            for place, part in enumerate(pair):
                rows = pl.ds((start + part) * lanes, lanes)
                weights[rows, :] = side_by_side(spread[:, place * lanes : (place + 1) * lanes] * same)


def weighted(pieces, weights, start):
    rows = pl.ds(start * lanes, len(pieces) * lanes)
    product = both_ways(dot(jnp.concatenate(pieces, axis=1), weights[rows, :]))
    half = product.shape[0] // 2
    return product[:half] + product[half:]


def convolve_kernel(sections, count_x, count_y, received, weights, blocks_far, blocks, left):
    columns = {}
    for level in (1, 2, 3):
        slices = len(block_rows[level])
        values = jnp.concatenate(
            [received[pl.ds(row, lanes, stride=rows_per_block), :] for row in block_rows[level]], axis=0
        )
        start, offsets = sections[level, 0]
        stack = jnp.concatenate(split(values), axis=0).reshape(2 * slices, count_x, count_y, lanes)
        pieces = []
        for offset in offsets:
            turn = offset % count_x
            turned = jnp.concatenate([stack[:, turn:], stack[:, :turn]], axis=1) if turn else stack
            pieces.append(turned.reshape(2 * slices * lanes, lanes))
        columns[level] = weighted(pieces, weights, start)
    for level in (1, 2, 3):
        slices = len(block_rows[level])
        start, offsets = sections[level, 1]
        stack = columns[level].reshape(slices * count_x, count_y, lanes)
        pieces = []
        for offset in offsets:
            turn = offset % count_y
            turned = jnp.concatenate([stack[:, turn:], stack[:, :turn]], axis=1) if turn else stack
            pieces.append(jnp.concatenate(split(turned.reshape(slices * lanes, lanes)), axis=0))
        values = weighted(pieces, weights, start)
        for index, row in enumerate(block_rows[level]):
            blocks[pl.ds(row, lanes, stride=rows_per_block), :] = values[lanes * index : lanes * (index + 1)]
    copies = []
    for index in range(4):
        section = pl.ds(224 * index, 224)
        copies.append(pltpu.make_async_copy(blocks.at[section], blocks_far.at[section], left.at[index]))
        copies[-1].start()
    for copy in copies:
        copy.wait()


def finish_kernel(received, constants, twice_up, finest, potential, ready, left):
    rows_x, rows_y, depth = finest.shape
    row_window = constants[:, 256:512]
    parts = {
        level: jnp.concatenate(
            [received[pl.ds(row, lanes, stride=rows_per_block), :] for row in block_rows[level]], axis=0
        )
        for level in (1, 2, 3)
    }
    coarsest = both_ways(dot(twice_up[...], side_by_side(parts[3])))
    pairs = wrapped(side_by_side(parts[2]), 64, 0)
    middle = jnp.concatenate(
        [both_ways(dot(row_window, pairs[begin : begin + 256])) for begin in (0, lanes)], axis=0
    )
    running = parts[1] + middle + coarsest
    pairs = wrapped(side_by_side(running), 64, 0)
    copies = []
    for index in range(depth // 256):
        fine = both_ways(dot(row_window, pairs[lanes * index : lanes * index + 256]))
        smooth = dot_lanes(constants[:, 0:256], side_by_side(fine))
        section = slice(256 * index, 256 * (index + 1))
        ready[:, :, section] = finest[:, :, section] + smooth.reshape(rows_x, rows_y, 256)
        places = pl.ds(256 * index, 256)
        copies.append(
            pltpu.make_async_copy(ready.at[:, :, places], potential.at[:, :, places], left.at[index])
        )
        copies[-1].start()
    for copy in copies:
        copy.wait()


def convolve_y_kernel(taps, before, own, after, summed_ref, head, tail):
    rows_x, rows_y, depth = own.shape
    for row in range(rows_x):
        lines = jnp.concatenate([before[row], own[row], after[row]], axis=0)
        summed = taps[1, 0, 0] * lines[0:rows_y]
        for tap in range(1, 9):
            summed = summed + taps[1, 0, tap] * lines[tap : tap + rows_y]
        summed_ref[row] = summed
        if row < 4:
            head[row] = summed
        if row >= rows_x - 4:
            tail[row - (rows_x - 4)] = summed


def convolve_xz_kernel(taps, before, own, after, result):
    rows_x, rows_y, depth = own.shape

    def layer(index):
        if index < 4:
            return before[index]
        return own[index - 4] if index < 4 + rows_x else after[index - 4 - rows_x]

    for row in range(rows_x):
        summed = taps[0, 0, 0] * layer(row)
        for tap in range(1, 9):
            summed = summed + taps[0, 0, tap] * layer(row + tap)
        total = taps[2, 0, 4] * summed
        for tap in (0, 1, 2, 3, 5, 6, 7, 8):
            total = total + taps[2, 0, tap] * pltpu.roll(summed, (4 - tap) % depth, 1)
        result[row] = total


def in_vmem(count):
    return [pl.BlockSpec(memory_space=pltpu.VMEM)] * count


scalars = pl.BlockSpec(memory_space=pltpu.SMEM)
far = pl.BlockSpec(memory_space=pltpu.HBM)


def shape_of(*shape, dtype=jnp.float32):
    return jax.ShapeDtypeStruct(shape, dtype)


def call(kernel, outs, in_specs, scratch=(), out_specs=None, limit=16, flops=0, moved=0):
    if out_specs is None:
        out_specs = jax.tree.map(lambda _: pl.BlockSpec(memory_space=pltpu.VMEM), outs)
    return pl.pallas_call(
        kernel,
        out_shape=outs,
        in_specs=in_specs,
        out_specs=out_specs,
        scratch_shapes=list(scratch),
        compiler_params=pltpu.CompilerParams(vmem_limit_bytes=limit * 2**20),
        cost_estimate=pl.CostEstimate(flops=flops, bytes_accessed=moved, transcendentals=0),
    )


def per_device(charges, kernel_taps):
    count_x, count_y = lax.axis_size("gx"), lax.axis_size("gy")
    rows_x, rows_y, depth = charges.shape
    taps = jnp.transpose(kernel_taps, (1, 0, 2))
    both = ("gx", "gy")
    down, up = restrict_1d(0), prolong_1d(0)
    down_constants = np.concatenate(
        [
            padded(np.kron(down, down), lanes, rows_x * rows_y),
            restrict_window(lanes, 512, 128),
            restrict_window(lanes, 384, 64),
        ],
        axis=1,
    )
    down_constants = jnp.asarray(down_constants, jnp.bfloat16)

    up_1 = padded(np.kron(up, up), rows_x * rows_y, lanes)
    up_constants = jnp.asarray(
        np.concatenate([up_1, up_1, prolong_window(256, 256, 64)], axis=1), jnp.bfloat16
    )
    twice_up = jnp.asarray(prolong_ring(4 * lanes) @ prolong_ring(2 * lanes), jnp.bfloat16)
    sections, section_count = weight_sections(count_x, count_y)
    block_shape = (lanes * rows_per_block, lanes)
    exchange_shape = (lanes * rows_per_block, 1, lanes)

    blocks, head, tail = call(
        restrict_kernel,
        (
            shape_of(*block_shape),
            shape_of(rows_x, 4, depth),
            shape_of(rows_x, 4, depth),
        ),
        [far] * 3,
        [
            pltpu.SMEM(taps.shape, jnp.float32),
            pltpu.VMEM((rows_x, rows_y, depth), jnp.float32),
            pltpu.VMEM(down_constants.shape, jnp.bfloat16),
            pltpu.VMEM((2 * lanes, depth + 2 * lanes), jnp.bfloat16),
            pltpu.VMEM((7 * lanes + 48, lanes), jnp.float32),
            pltpu.VMEM(block_shape, jnp.float32),
            pltpu.SemaphoreType.DMA((8 + depth // 256,)),
        ],
        (far,) * 3,
        limit=60,
        flops=10**9,
        moved=2 * 10**6,
    )(taps, charges, down_constants)
    received = lax.all_to_all(blocks.reshape(exchange_shape), both, 0, 0, tiled=True)

    weights = call(
        lambda *refs: weight_kernel(sections, *refs),
        shape_of(section_count * lanes, 2 * lanes, dtype=jnp.bfloat16),
        [scalars] + in_vmem(1),
        flops=2 * 10**7,
        moved=3 * 10**6,
    )(taps, tap_tables())

    def shifted(values, axis, step):
        count = lax.axis_size(axis)
        return lax.ppermute(values, axis, [(i, (i + step) % count) for i in range(count)])

    before = shifted(tail, "gy", 1)
    after = shifted(head, "gy", -1)
    summed, head, tail = call(
        convolve_y_kernel,
        (shape_of(rows_x, rows_y, depth), shape_of(4, rows_y, depth), shape_of(4, rows_y, depth)),
        [scalars] + in_vmem(3),
        flops=10**11,
        moved=3 * 10**6,
    )(taps, before, charges, after)
    received, _ = lax.optimization_barrier((received, tail))
    finest = call(
        convolve_xz_kernel,
        shape_of(rows_x, rows_y, depth),
        [scalars] + in_vmem(3),
        flops=10**11,
        moved=3 * 10**6,
    )(taps, shifted(tail, "gx", 1), summed, shifted(head, "gx", -1))

    blocks = call(
        lambda *refs: convolve_kernel(sections, count_x, count_y, *refs),
        shape_of(*block_shape),
        in_vmem(2),
        [pltpu.VMEM(block_shape, jnp.float32), pltpu.SemaphoreType.DMA((4,))],
        far,
        flops=10**9,
        moved=4 * 10**6,
    )(received.reshape(block_shape), weights)
    received = lax.all_to_all(blocks.reshape(exchange_shape), both, 0, 0, tiled=True)

    return call(
        finish_kernel,
        shape_of(rows_x, rows_y, depth),
        in_vmem(4),
        [pltpu.VMEM((rows_x, rows_y, depth), jnp.float32), pltpu.SemaphoreType.DMA((depth // 256,))],
        far,
        flops=10**9,
        moved=4 * 10**6,
    )(received.reshape(block_shape), up_constants, twice_up, finest)


def solution(mesh):
    placed = (P("gx", "gy", None), P())
    return jax.shard_map(
        per_device, mesh=mesh, in_specs=placed, out_specs=P("gx", "gy", None), check_vma=False
    )
```

```python
import jax
import jax.numpy as jnp
import numpy as np
from jax import lax
from jax.experimental import pallas as pl
from jax.experimental.pallas import tpu as pltpu
from jax.sharding import PartitionSpec as P

first_cell = (0, -1, -2, -2)
cell_count = (16, 11, 9, 7)
brick_cells = (16, 8, 4, 2)
restrict_taps = {-3: -0.0625, -1: 0.5625, 0: 1.0, 1: 0.5625, 3: -0.0625}
lanes = 128
block_rows = ((), (0, 1, 2, 3), (4, 5), (6,))
rows_per_block = 7


def restrict_1d(level):
    matrix = np.zeros((cell_count[level + 1], cell_count[level]), np.float32)
    for coarse in range(cell_count[level + 1]):
        for fine in range(cell_count[level]):
            offset = first_cell[level] + fine - 2 * (first_cell[level + 1] + coarse)
            matrix[coarse, fine] = restrict_taps.get(offset, 0.0)
    return matrix


def prolong_entries(fine):
    if fine % 2 == 0:
        return {fine // 2: 1.0}
    left = (fine - 1) // 2
    return {left - 1: -0.0625, left: 0.5625, left + 1: 0.5625, left + 2: -0.0625}


def prolong_1d(level):
    matrix = np.zeros((cell_count[level], cell_count[level + 1]), np.float32)
    for fine in range(cell_count[level]):
        for coarse, weight in prolong_entries(first_cell[level] + fine).items():
            matrix[fine, coarse - first_cell[level + 1]] = weight
    return matrix


def padded(matrix, rows, columns):
    result = np.zeros((rows, columns), np.float32)
    result[: matrix.shape[0], : matrix.shape[1]] = matrix
    return result


def restrict_window(rows, width, margin):
    matrix = np.zeros((rows, width), np.float32)
    for coarse in range(rows):
        for offset, weight in restrict_taps.items():
            matrix[coarse, margin + 2 * coarse + offset] = weight
    return matrix


def prolong_window(rows, width, margin):
    matrix = np.zeros((rows, width), np.float32)
    for fine in range(rows):
        for coarse, weight in prolong_entries(fine).items():
            matrix[fine, margin + coarse] = weight
    return matrix


def prolong_ring(rows):
    matrix = np.zeros((rows, rows // 2), np.float32)
    for fine in range(rows):
        for coarse, weight in prolong_entries(fine).items():
            matrix[fine, coarse % (rows // 2)] = weight
    return matrix


def to_level(level):
    down = up = np.eye(cell_count[1], dtype=np.float32)
    for step in range(1, level):
        down, up = restrict_1d(step) @ down, up @ prolong_1d(step)
    return down, up


def tap_tables():
    count = cell_count[1]
    cells = [divmod(cell, count) for cell in range(count * count)]
    tables = []
    for axis in (0, 1):
        same = np.zeros((lanes, lanes), np.float32)
        for row, here in enumerate(cells):
            for column, there in enumerate(cells):
                same[row, column] = here[1 - axis] == there[1 - axis]
        tables.append(same)
    for level in (1, 2, 3):
        down, up = to_level(level)
        size = cell_count[level]
        for axis in (0, 1):
            into, out_of = np.zeros((lanes, lanes), np.float32), np.zeros((16, lanes), np.float32)
            number = np.full((16, lanes), 256.0, np.float32)
            for cell, place in enumerate(cells):
                into[cell, :size] = down[:, place[axis]]
                out_of[:size, cell] = up[place[axis], :]
            for source in range(size):
                for wanted in range(size):
                    number[source, wanted] = source - wanted + 4
            tables += [into, out_of, number]
    return jnp.asarray(np.concatenate(tables), jnp.bfloat16)


def brick_offsets(level, axis, bricks):
    if level == 3 and axis == 0:
        return tuple(range(bricks))
    reach = {1: 1, 2: 3, 3: 5}[level]
    return tuple(range(-reach, reach + 1))


def weight_sections(count_x, count_y):
    sections, start = {}, 0
    for level in (1, 2, 3):
        for axis, bricks in ((0, count_x), (1, count_y)):
            offsets = brick_offsets(level, axis, bricks)
            sections[level, axis] = (start, offsets)
            start += len(offsets)
    return sections, start


def split(values):
    high = values.astype(jnp.bfloat16)
    return high, (values - high.astype(jnp.float32)).astype(jnp.bfloat16)


def dot(left, right):
    return lax.dot_general(left, right, (((1,), (0,)), ((), ())), preferred_element_type=jnp.float32)


def dot_lanes(left, right):
    return lax.dot_general(left, right, (((1,), (1,)), ((), ())), preferred_element_type=jnp.float32)


def wrapped(values, margin, axis):
    size = values.shape[axis]
    tail = lax.slice_in_dim(values, size - margin, size, axis=axis)
    head = lax.slice_in_dim(values, 0, margin, axis=axis)
    return jnp.concatenate([tail, values, head], axis=axis)


def both_ways(product):
    half = product.shape[1] // 2
    return product[:, :half] + product[:, half:]


def side_by_side(values):
    return jnp.concatenate(split(values), axis=1)


def restrict_kernel(
    taps_far, charges_far, constants_far, blocks_far, head, tail, taps, charges, constants, patch, rim, blocks, arrived
):
    rows_x, rows_y, depth = charges.shape
    columns = rows_x * rows_y
    copies = [
        pltpu.make_async_copy(constants_far, constants, arrived.at[0]),
        pltpu.make_async_copy(taps_far, taps, arrived.at[1]),
    ]
    leaving = [
        pltpu.make_async_copy(charges.at[:, pl.ds(0, 4)], head, arrived.at[2]),
        pltpu.make_async_copy(charges.at[:, pl.ds(rows_y - 4, 4)], tail, arrived.at[3]),
    ]
    chunks = []
    for index in range(depth // 256):
        section = pl.ds(256 * index, 256)
        chunks.append(
            pltpu.make_async_copy(
                charges_far.at[:, :, section], charges.at[:, :, section], arrived.at[4 + index]
            )
        )
    copies[0].start()
    for chunk in chunks:
        chunk.start()
    copies[1].start()
    copies[0].wait()
    for index, chunk in enumerate(chunks):
        chunk.wait()
        high, low = split(charges[:, :, 256 * index : 256 * (index + 1)].reshape(columns, 256))
        down = constants[:, 0:columns]
        high, low = split(dot(down, high) + dot(down, low))
        begin = lanes + 256 * index
        patch[0:lanes, begin : begin + 256] = high
        patch[lanes : 2 * lanes, begin : begin + 256] = low
    for copy in leaving:
        copy.start()
    patch[:, 0:lanes] = patch[:, depth : depth + lanes]
    patch[:, depth + lanes : depth + 2 * lanes] = patch[:, lanes : 2 * lanes]
    lane_window = constants[:, 256:768]
    row_window = constants[:, 768:1152]
    grid = jnp.concatenate(
        [
            both_ways(dot_lanes(lane_window, patch[:, begin : begin + 512]))
            for begin in range(0, depth, 256)
        ],
        axis=0,
    )
    grids = {1: grid}
    for level in (1, 2):
        ready = wrapped(side_by_side(grid), 64, 0)
        grid = jnp.concatenate(
            [
                both_ways(dot(row_window, ready[begin : begin + 384]))
                for begin in range(0, grid.shape[0], 256)
            ],
            axis=0,
        )
        grids[level + 1] = grid
    copies[1].wait()
    firsts, first = {}, 0
    for level in (1, 2, 3):
        grid = grids[level]
        cells = grid.shape[0]
        rim[first : first + 8, :] = grid[cells - 8 :, :]
        rim[first + 8 : first + 8 + cells, :] = grid
        rim[first + 8 + cells : first + 16 + cells, :] = grid[:8, :]
        firsts[level] = first
        first += cells + 16
    share = lanes // 4
    for part in range(4):
        for level in (1, 2, 3):
            for index, row in enumerate(block_rows[level]):
                summed = None
                for tap in range(9):
                    begin = firsts[level] + lanes * index + share * part + 4 + tap
                    term = taps[2, level, tap] * rim[begin : begin + share, :]
                    summed = term if summed is None else summed + term
                blocks[pl.ds(rows_per_block * share * part + row, share, stride=rows_per_block), :] = summed
        section = pl.ds(rows_per_block * share * part, rows_per_block * share)
        leaving.append(
            pltpu.make_async_copy(blocks.at[section], blocks_far.at[section], arrived.at[4 + depth // 256 + part])
        )
        leaving[-1].start()
    for copy in leaving:
        copy.wait()


def weight_kernel(sections, taps, tables, weights):
    tables_at = {
        (level, axis): 2 * lanes + (2 * (level - 1) + axis) * (lanes + 32) for level, axis in sections
    }
    stacks = {}
    for (level, axis), (start, offsets) in sections.items():
        begin = tables_at[level, axis] + lanes + 16
        base = tables[begin : begin + 16, :].astype(jnp.float32).astype(jnp.int32)
        scale = 0.5**level if axis == 0 else 1.0
        values = [scale * taps[axis, level, tap] for tap in range(9)]
        stack = []
        for offset in offsets:
            number = base + brick_cells[level] * offset
            if level == 3 and axis == 0:
                number = number & 271
            chosen = jnp.zeros(number.shape, jnp.float32)
            for tap in range(9):
                chosen = jnp.where(number == tap, values[tap], chosen)
            stack.append(chosen)
        stacks[level, axis] = split(jnp.concatenate(stack, axis=0))
    for level, axis in sections:
        begin = tables_at[level, axis] + lanes
        high, low = stacks[level, axis]
        out_of = tables[begin : begin + 16, :]
        stacks[level, axis] = split(dot(high[:, 0:16], out_of) + dot(low[:, 0:16], out_of))
    for (level, axis), (start, offsets) in sections.items():
        same = tables[axis * lanes : (axis + 1) * lanes, :].astype(jnp.float32)
        into = tables[tables_at[level, axis] : tables_at[level, axis] + lanes, 0:16]
        into = jnp.concatenate([into, into], axis=1)
        for index in range(0, len(offsets), 2):
            pair = range(index, min(index + 2, len(offsets)))
            parts = [
                jnp.concatenate([half[16 * part : 16 * (part + 1)] for part in pair], axis=1)
                for half in stacks[level, axis]
            ]
            spread = dot(into, jnp.concatenate(parts, axis=0))
            for place, part in enumerate(pair):
                rows = pl.ds((start + part) * lanes, lanes)
                weights[rows, :] = side_by_side(spread[:, place * lanes : (place + 1) * lanes] * same)


def weighted(pieces, weights, start):
    rows = pl.ds(start * lanes, len(pieces) * lanes)
    product = both_ways(dot(jnp.concatenate(pieces, axis=1), weights[rows, :]))
    half = product.shape[0] // 2
    return product[:half] + product[half:]


def convolve_kernel(sections, count_x, count_y, received, weights, blocks_far, blocks, left):
    columns = {}
    for level in (1, 2, 3):
        slices = len(block_rows[level])
        values = jnp.concatenate(
            [received[pl.ds(row, lanes, stride=rows_per_block), :] for row in block_rows[level]], axis=0
        )
        start, offsets = sections[level, 0]
        stack = jnp.concatenate(split(values), axis=0).reshape(2 * slices, count_x, count_y, lanes)
        pieces = []
        for offset in offsets:
            turn = offset % count_x
            turned = jnp.concatenate([stack[:, turn:], stack[:, :turn]], axis=1) if turn else stack
            pieces.append(turned.reshape(2 * slices * lanes, lanes))
        columns[level] = weighted(pieces, weights, start)
    for level in (1, 2, 3):
        slices = len(block_rows[level])
        start, offsets = sections[level, 1]
        stack = columns[level].reshape(slices * count_x, count_y, lanes)
        pieces = []
        for offset in offsets:
            turn = offset % count_y
            turned = jnp.concatenate([stack[:, turn:], stack[:, :turn]], axis=1) if turn else stack
            pieces.append(jnp.concatenate(split(turned.reshape(slices * lanes, lanes)), axis=0))
        values = weighted(pieces, weights, start)
        for index, row in enumerate(block_rows[level]):
            blocks[pl.ds(row, lanes, stride=rows_per_block), :] = values[lanes * index : lanes * (index + 1)]
    copies = []
    for index in range(4):
        section = pl.ds(224 * index, 224)
        copies.append(pltpu.make_async_copy(blocks.at[section], blocks_far.at[section], left.at[index]))
        copies[-1].start()
    for copy in copies:
        copy.wait()


def finish_kernel(received, constants, twice_up, finest, potential, ready, left):
    rows_x, rows_y, depth = finest.shape
    row_window = constants[:, 256:512]
    parts = {
        level: jnp.concatenate(
            [received[pl.ds(row, lanes, stride=rows_per_block), :] for row in block_rows[level]], axis=0
        )
        for level in (1, 2, 3)
    }
    coarsest = both_ways(dot(twice_up[...], side_by_side(parts[3])))
    pairs = wrapped(side_by_side(parts[2]), 64, 0)
    middle = jnp.concatenate(
        [both_ways(dot(row_window, pairs[begin : begin + 256])) for begin in (0, lanes)], axis=0
    )
    running = parts[1] + middle + coarsest
    pairs = wrapped(side_by_side(running), 64, 0)
    copies = []
    for index in range(depth // 256):
        fine = both_ways(dot(row_window, pairs[lanes * index : lanes * index + 256]))
        smooth = dot_lanes(constants[:, 0:256], side_by_side(fine))
        section = slice(256 * index, 256 * (index + 1))
        ready[:, :, section] = finest[:, :, section] + smooth.reshape(rows_x, rows_y, 256)
        places = pl.ds(256 * index, 256)
        copies.append(
            pltpu.make_async_copy(ready.at[:, :, places], potential.at[:, :, places], left.at[index])
        )
        copies[-1].start()
    for copy in copies:
        copy.wait()


def along_y(taps, before, own, after, row):
    rows_y = own.shape[1]
    lines = jnp.concatenate([before[row], own[row], after[row]], axis=0)
    summed = taps[1, 0, 0] * lines[0:rows_y]
    for tap in range(1, 9):
        summed = summed + taps[1, 0, tap] * lines[tap : tap + rows_y]
    return summed


def edge_kernel(taps, before, own, after, head, tail):
    rows_x = own.shape[0]
    for row in range(4):
        head[row] = along_y(taps, before, own, after, row)
        tail[row] = along_y(taps, before, own, after, rows_x - 4 + row)


def finest_kernel(taps, before_y, own, after_y, before, after, result, summed_y):
    rows_x, rows_y, depth = own.shape
    for row in range(rows_x):
        summed_y[row] = along_y(taps, before_y, own, after_y, row)

    def layer(index):
        if index < 4:
            return before[index]
        return summed_y[index - 4] if index < 4 + rows_x else after[index - 4 - rows_x]

    for row in range(rows_x):
        summed = taps[0, 0, 0] * layer(row)
        for tap in range(1, 9):
            summed = summed + taps[0, 0, tap] * layer(row + tap)
        total = taps[2, 0, 4] * summed
        for tap in (0, 1, 2, 3, 5, 6, 7, 8):
            total = total + taps[2, 0, tap] * pltpu.roll(summed, (4 - tap) % depth, 1)
        result[row] = total


def in_vmem(count):
    return [pl.BlockSpec(memory_space=pltpu.VMEM)] * count


scalars = pl.BlockSpec(memory_space=pltpu.SMEM)
far = pl.BlockSpec(memory_space=pltpu.HBM)


def shape_of(*shape, dtype=jnp.float32):
    return jax.ShapeDtypeStruct(shape, dtype)


def call(kernel, outs, in_specs, scratch=(), out_specs=None, limit=16, flops=0, moved=0):
    if out_specs is None:
        out_specs = jax.tree.map(lambda _: pl.BlockSpec(memory_space=pltpu.VMEM), outs)
    return pl.pallas_call(
        kernel,
        out_shape=outs,
        in_specs=in_specs,
        out_specs=out_specs,
        scratch_shapes=list(scratch),
        compiler_params=pltpu.CompilerParams(vmem_limit_bytes=limit * 2**20),
        cost_estimate=pl.CostEstimate(flops=flops, bytes_accessed=moved, transcendentals=0),
    )


def per_device(charges, kernel_taps):
    count_x, count_y = lax.axis_size("gx"), lax.axis_size("gy")
    rows_x, rows_y, depth = charges.shape
    taps = jnp.transpose(kernel_taps, (1, 0, 2))
    both = ("gx", "gy")
    down, up = restrict_1d(0), prolong_1d(0)
    down_constants = np.concatenate(
        [
            padded(np.kron(down, down), lanes, rows_x * rows_y),
            restrict_window(lanes, 512, 128),
            restrict_window(lanes, 384, 64),
        ],
        axis=1,
    )
    down_constants = jnp.asarray(down_constants, jnp.bfloat16)

    up_1 = padded(np.kron(up, up), rows_x * rows_y, lanes)
    up_constants = jnp.asarray(
        np.concatenate([up_1, up_1, prolong_window(256, 256, 64)], axis=1), jnp.bfloat16
    )
    twice_up = jnp.asarray(prolong_ring(4 * lanes) @ prolong_ring(2 * lanes), jnp.bfloat16)
    sections, section_count = weight_sections(count_x, count_y)
    block_shape = (lanes * rows_per_block, lanes)
    exchange_shape = (lanes * rows_per_block, 1, lanes)

    blocks, head, tail = call(
        restrict_kernel,
        (
            shape_of(*block_shape),
            shape_of(rows_x, 4, depth),
            shape_of(rows_x, 4, depth),
        ),
        [far] * 3,
        [
            pltpu.SMEM(taps.shape, jnp.float32),
            pltpu.VMEM((rows_x, rows_y, depth), jnp.float32),
            pltpu.VMEM(down_constants.shape, jnp.bfloat16),
            pltpu.VMEM((2 * lanes, depth + 2 * lanes), jnp.bfloat16),
            pltpu.VMEM((7 * lanes + 48, lanes), jnp.float32),
            pltpu.VMEM(block_shape, jnp.float32),
            pltpu.SemaphoreType.DMA((8 + depth // 256,)),
        ],
        (far,) * 3,
        limit=60,
        flops=10**9,
        moved=2 * 10**6,
    )(taps, charges, down_constants)
    received = lax.all_to_all(blocks.reshape(exchange_shape), both, 0, 0, tiled=True)

    weights = call(
        lambda *refs: weight_kernel(sections, *refs),
        shape_of(section_count * lanes, 2 * lanes, dtype=jnp.bfloat16),
        [scalars] + in_vmem(1),
        flops=2 * 10**7,
        moved=3 * 10**6,
    )(taps, tap_tables())

    def shifted(values, axis, step):
        count = lax.axis_size(axis)
        return lax.ppermute(values, axis, [(i, (i + step) % count) for i in range(count)])

    before = shifted(tail, "gy", 1)
    after = shifted(head, "gy", -1)
    head, tail = call(
        edge_kernel,
        (shape_of(4, rows_y, depth), shape_of(4, rows_y, depth)),
        [scalars] + in_vmem(3),
        flops=10**11,
        moved=3 * 10**6,
    )(taps, before, charges, after)
    received, _ = lax.optimization_barrier((received, tail))
    finest = call(
        finest_kernel,
        shape_of(rows_x, rows_y, depth),
        [scalars] + in_vmem(5),
        [pltpu.VMEM((rows_x, rows_y, depth), jnp.float32)],
        flops=10**11,
        moved=3 * 10**6,
    )(taps, before, charges, after, shifted(tail, "gx", 1), shifted(head, "gx", -1))

    blocks = call(
        lambda *refs: convolve_kernel(sections, count_x, count_y, *refs),
        shape_of(*block_shape),
        in_vmem(2),
        [pltpu.VMEM(block_shape, jnp.float32), pltpu.SemaphoreType.DMA((4,))],
        far,
        flops=10**9,
        moved=4 * 10**6,
    )(received.reshape(block_shape), weights)
    received = lax.all_to_all(blocks.reshape(exchange_shape), both, 0, 0, tiled=True)

    return call(
        finish_kernel,
        shape_of(rows_x, rows_y, depth),
        in_vmem(4),
        [pltpu.VMEM((rows_x, rows_y, depth), jnp.float32), pltpu.SemaphoreType.DMA((depth // 256,))],
        far,
        flops=10**9,
        moved=4 * 10**6,
    )(received.reshape(block_shape), up_constants, twice_up, finest)


def solution(mesh):
    placed = (P("gx", "gy", None), P())
    return jax.shard_map(
        per_device, mesh=mesh, in_specs=placed, out_specs=P("gx", "gy", None), check_vma=False
    )
```

```python
import jax
import jax.numpy as jnp
import numpy as np
from jax import lax
from jax.experimental import pallas as pl
from jax.experimental.pallas import tpu as pltpu
from jax.sharding import PartitionSpec as P

first_cell = (0, -1, -2, -2)
cell_count = (16, 11, 9, 7)
brick_cells = (16, 8, 4, 2)
restrict_taps = {-3: -0.0625, -1: 0.5625, 0: 1.0, 1: 0.5625, 3: -0.0625}
lanes = 128
block_rows = ((), (0, 1, 2, 3), (4, 5), (6,))
rows_per_block = 7


def restrict_1d(level):
    matrix = np.zeros((cell_count[level + 1], cell_count[level]), np.float32)
    for coarse in range(cell_count[level + 1]):
        for fine in range(cell_count[level]):
            offset = first_cell[level] + fine - 2 * (first_cell[level + 1] + coarse)
            matrix[coarse, fine] = restrict_taps.get(offset, 0.0)
    return matrix


def prolong_entries(fine):
    if fine % 2 == 0:
        return {fine // 2: 1.0}
    left = (fine - 1) // 2
    return {left - 1: -0.0625, left: 0.5625, left + 1: 0.5625, left + 2: -0.0625}


def prolong_1d(level):
    matrix = np.zeros((cell_count[level], cell_count[level + 1]), np.float32)
    for fine in range(cell_count[level]):
        for coarse, weight in prolong_entries(first_cell[level] + fine).items():
            matrix[fine, coarse - first_cell[level + 1]] = weight
    return matrix


def padded(matrix, rows, columns):
    result = np.zeros((rows, columns), np.float32)
    result[: matrix.shape[0], : matrix.shape[1]] = matrix
    return result


def restrict_window(rows, width, margin):
    matrix = np.zeros((rows, width), np.float32)
    for coarse in range(rows):
        for offset, weight in restrict_taps.items():
            matrix[coarse, margin + 2 * coarse + offset] = weight
    return matrix


def prolong_window(rows, width, margin):
    matrix = np.zeros((rows, width), np.float32)
    for fine in range(rows):
        for coarse, weight in prolong_entries(fine).items():
            matrix[fine, margin + coarse] = weight
    return matrix


def prolong_ring(rows):
    matrix = np.zeros((rows, rows // 2), np.float32)
    for fine in range(rows):
        for coarse, weight in prolong_entries(fine).items():
            matrix[fine, coarse % (rows // 2)] = weight
    return matrix


def to_level(level):
    down = up = np.eye(cell_count[1], dtype=np.float32)
    for step in range(1, level):
        down, up = restrict_1d(step) @ down, up @ prolong_1d(step)
    return down, up


def tap_tables():
    count = cell_count[1]
    cells = [divmod(cell, count) for cell in range(count * count)]
    tables = []
    for axis in (0, 1):
        same = np.zeros((lanes, lanes), np.float32)
        for row, here in enumerate(cells):
            for column, there in enumerate(cells):
                same[row, column] = here[1 - axis] == there[1 - axis]
        tables.append(same)
    for level in (1, 2, 3):
        down, up = to_level(level)
        size = cell_count[level]
        for axis in (0, 1):
            into, out_of = np.zeros((lanes, lanes), np.float32), np.zeros((16, lanes), np.float32)
            number = np.full((16, lanes), 256.0, np.float32)
            for cell, place in enumerate(cells):
                into[cell, :size] = down[:, place[axis]]
                out_of[:size, cell] = up[place[axis], :]
            for source in range(size):
                for wanted in range(size):
                    number[source, wanted] = source - wanted + 4
            tables += [into, out_of, number]
    return jnp.asarray(np.concatenate(tables), jnp.bfloat16)


def brick_offsets(level, axis, bricks):
    if level == 3 and axis == 0:
        return tuple(range(bricks))
    reach = {1: 1, 2: 3, 3: 5}[level]
    return tuple(range(-reach, reach + 1))


def weight_sections(count_x, count_y):
    sections, start = {}, 0
    for level in (1, 2, 3):
        for axis, bricks in ((0, count_x), (1, count_y)):
            offsets = brick_offsets(level, axis, bricks)
            sections[level, axis] = (start, offsets)
            start += len(offsets)
    return sections, start


def split(values):
    high = values.astype(jnp.bfloat16)
    return high, (values - high.astype(jnp.float32)).astype(jnp.bfloat16)


def dot(left, right):
    return lax.dot_general(left, right, (((1,), (0,)), ((), ())), preferred_element_type=jnp.float32)


def dot_lanes(left, right):
    return lax.dot_general(left, right, (((1,), (1,)), ((), ())), preferred_element_type=jnp.float32)


def wrapped(values, margin, axis):
    size = values.shape[axis]
    tail = lax.slice_in_dim(values, size - margin, size, axis=axis)
    head = lax.slice_in_dim(values, 0, margin, axis=axis)
    return jnp.concatenate([tail, values, head], axis=axis)


def both_ways(product):
    half = product.shape[1] // 2
    return product[:, :half] + product[:, half:]


def side_by_side(values):
    return jnp.concatenate(split(values), axis=1)


def restrict_kernel(
    taps_far, charges_far, constants_far, blocks_far, head, tail, taps, charges, constants, patch, rim, blocks, arrived
):
    rows_x, rows_y, depth = charges.shape
    columns = rows_x * rows_y
    copies = [
        pltpu.make_async_copy(
            constants_far.at[:, pl.ds(0, columns)], constants.at[:, pl.ds(0, columns)], arrived.at[0]
        ),
        pltpu.make_async_copy(taps_far, taps, arrived.at[1]),
        pltpu.make_async_copy(
            constants_far.at[:, pl.ds(columns, 896)],
            constants.at[:, pl.ds(columns, 896)],
            arrived.at[8 + depth // 256],
        ),
    ]
    leaving = [
        pltpu.make_async_copy(charges.at[:, pl.ds(0, 4)], head, arrived.at[2]),
        pltpu.make_async_copy(charges.at[:, pl.ds(rows_y - 4, 4)], tail, arrived.at[3]),
    ]
    chunks = []
    for index in range(depth // 256):
        section = pl.ds(256 * index, 256)
        chunks.append(
            pltpu.make_async_copy(
                charges_far.at[:, :, section], charges.at[:, :, section], arrived.at[4 + index]
            )
        )
    copies[0].start()
    for chunk in chunks:
        chunk.start()
    copies[1].start()
    copies[2].start()
    copies[0].wait()
    for index, chunk in enumerate(chunks):
        chunk.wait()
        high, low = split(charges[:, :, 256 * index : 256 * (index + 1)].reshape(columns, 256))
        down = constants[:, 0:columns]
        high, low = split(dot(down, high) + dot(down, low))
        begin = lanes + 256 * index
        patch[0:lanes, begin : begin + 256] = high
        patch[lanes : 2 * lanes, begin : begin + 256] = low
    for copy in leaving:
        copy.start()
    patch[:, 0:lanes] = patch[:, depth : depth + lanes]
    patch[:, depth + lanes : depth + 2 * lanes] = patch[:, lanes : 2 * lanes]
    copies[2].wait()
    lane_window = constants[:, 256:768]
    row_window = constants[:, 768:1152]
    grid = jnp.concatenate(
        [
            both_ways(dot_lanes(lane_window, patch[:, begin : begin + 512]))
            for begin in range(0, depth, 256)
        ],
        axis=0,
    )
    grids = {1: grid}
    for level in (1, 2):
        ready = wrapped(side_by_side(grid), 64, 0)
        grid = jnp.concatenate(
            [
                both_ways(dot(row_window, ready[begin : begin + 384]))
                for begin in range(0, grid.shape[0], 256)
            ],
            axis=0,
        )
        grids[level + 1] = grid
    copies[1].wait()
    firsts, first = {}, 0
    for level in (1, 2, 3):
        grid = grids[level]
        cells = grid.shape[0]
        rim[first : first + 8, :] = grid[cells - 8 :, :]
        rim[first + 8 : first + 8 + cells, :] = grid
        rim[first + 8 + cells : first + 16 + cells, :] = grid[:8, :]
        firsts[level] = first
        first += cells + 16
    share = lanes // 4
    for part in range(4):
        for level in (1, 2, 3):
            for index, row in enumerate(block_rows[level]):
                summed = None
                for tap in range(9):
                    begin = firsts[level] + lanes * index + share * part + 4 + tap
                    term = taps[2, level, tap] * rim[begin : begin + share, :]
                    summed = term if summed is None else summed + term
                blocks[pl.ds(rows_per_block * share * part + row, share, stride=rows_per_block), :] = summed
        section = pl.ds(rows_per_block * share * part, rows_per_block * share)
        leaving.append(
            pltpu.make_async_copy(blocks.at[section], blocks_far.at[section], arrived.at[4 + depth // 256 + part])
        )
        leaving[-1].start()
    for copy in leaving:
        copy.wait()


def weight_kernel(sections, taps, tables, weights):
    tables_at = {
        (level, axis): 2 * lanes + (2 * (level - 1) + axis) * (lanes + 32) for level, axis in sections
    }
    stacks = {}
    for (level, axis), (start, offsets) in sections.items():
        begin = tables_at[level, axis] + lanes + 16
        base = tables[begin : begin + 16, :].astype(jnp.float32).astype(jnp.int32)
        scale = 0.5**level if axis == 0 else 1.0
        values = [scale * taps[axis, level, tap] for tap in range(9)]
        stack = []
        for offset in offsets:
            number = base + brick_cells[level] * offset
            if level == 3 and axis == 0:
                number = number & 271
            chosen = jnp.zeros(number.shape, jnp.float32)
            for tap in range(9):
                chosen = jnp.where(number == tap, values[tap], chosen)
            stack.append(chosen)
        stacks[level, axis] = split(jnp.concatenate(stack, axis=0))
    for level, axis in sections:
        begin = tables_at[level, axis] + lanes
        high, low = stacks[level, axis]
        out_of = tables[begin : begin + 16, :]
        stacks[level, axis] = split(dot(high[:, 0:16], out_of) + dot(low[:, 0:16], out_of))
    for (level, axis), (start, offsets) in sections.items():
        same = tables[axis * lanes : (axis + 1) * lanes, :].astype(jnp.float32)
        into = tables[tables_at[level, axis] : tables_at[level, axis] + lanes, 0:16]
        into = jnp.concatenate([into, into], axis=1)
        for index in range(0, len(offsets), 2):
            pair = range(index, min(index + 2, len(offsets)))
            parts = [
                jnp.concatenate([half[16 * part : 16 * (part + 1)] for part in pair], axis=1)
                for half in stacks[level, axis]
            ]
            spread = dot(into, jnp.concatenate(parts, axis=0))
            for place, part in enumerate(pair):
                rows = pl.ds((start + part) * lanes, lanes)
                weights[rows, :] = side_by_side(spread[:, place * lanes : (place + 1) * lanes] * same)


def weighted(pieces, weights, start):
    rows = pl.ds(start * lanes, len(pieces) * lanes)
    product = both_ways(dot(jnp.concatenate(pieces, axis=1), weights[rows, :]))
    half = product.shape[0] // 2
    return product[:half] + product[half:]


def convolve_kernel(sections, count_x, count_y, received, weights, blocks_far, blocks, left):
    columns = {}
    for level in (1, 2, 3):
        slices = len(block_rows[level])
        values = jnp.concatenate(
            [received[pl.ds(row, lanes, stride=rows_per_block), :] for row in block_rows[level]], axis=0
        )
        start, offsets = sections[level, 0]
        stack = jnp.concatenate(split(values), axis=0).reshape(2 * slices, count_x, count_y, lanes)
        pieces = []
        for offset in offsets:
            turn = offset % count_x
            turned = jnp.concatenate([stack[:, turn:], stack[:, :turn]], axis=1) if turn else stack
            pieces.append(turned.reshape(2 * slices * lanes, lanes))
        columns[level] = weighted(pieces, weights, start)
    for level in (1, 2, 3):
        slices = len(block_rows[level])
        start, offsets = sections[level, 1]
        stack = columns[level].reshape(slices * count_x, count_y, lanes)
        pieces = []
        for offset in offsets:
            turn = offset % count_y
            turned = jnp.concatenate([stack[:, turn:], stack[:, :turn]], axis=1) if turn else stack
            pieces.append(jnp.concatenate(split(turned.reshape(slices * lanes, lanes)), axis=0))
        values = weighted(pieces, weights, start)
        for index, row in enumerate(block_rows[level]):
            blocks[pl.ds(row, lanes, stride=rows_per_block), :] = values[lanes * index : lanes * (index + 1)]
    copies = []
    for index in range(4):
        section = pl.ds(224 * index, 224)
        copies.append(pltpu.make_async_copy(blocks.at[section], blocks_far.at[section], left.at[index]))
        copies[-1].start()
    for copy in copies:
        copy.wait()


def finish_kernel(received, constants, twice_up, finest, potential, ready, left):
    rows_x, rows_y, depth = finest.shape
    row_window = constants[:, 256:512]
    parts = {
        level: jnp.concatenate(
            [received[pl.ds(row, lanes, stride=rows_per_block), :] for row in block_rows[level]], axis=0
        )
        for level in (1, 2, 3)
    }
    coarsest = both_ways(dot(twice_up[...], side_by_side(parts[3])))
    pairs = wrapped(side_by_side(parts[2]), 64, 0)
    middle = jnp.concatenate(
        [both_ways(dot(row_window, pairs[begin : begin + 256])) for begin in (0, lanes)], axis=0
    )
    running = parts[1] + middle + coarsest
    pairs = wrapped(side_by_side(running), 64, 0)
    copies = []
    for index in range(depth // 256):
        fine = both_ways(dot(row_window, pairs[lanes * index : lanes * index + 256]))
        smooth = dot_lanes(constants[:, 0:256], side_by_side(fine))
        section = slice(256 * index, 256 * (index + 1))
        ready[:, :, section] = finest[:, :, section] + smooth.reshape(rows_x, rows_y, 256)
        places = pl.ds(256 * index, 256)
        copies.append(
            pltpu.make_async_copy(ready.at[:, :, places], potential.at[:, :, places], left.at[index])
        )
        copies[-1].start()
    for copy in copies:
        copy.wait()


def along_y(taps, before, own, after, row):
    rows_y = own.shape[1]
    lines = jnp.concatenate([before[row], own[row], after[row]], axis=0)
    summed = taps[1, 0, 0] * lines[0:rows_y]
    for tap in range(1, 9):
        summed = summed + taps[1, 0, tap] * lines[tap : tap + rows_y]
    return summed


def edge_kernel(taps, before, own, after, head, tail):
    rows_x = own.shape[0]
    for row in range(4):
        head[row] = along_y(taps, before, own, after, row)
        tail[row] = along_y(taps, before, own, after, rows_x - 4 + row)


def finest_kernel(taps, before_y, own, after_y, before, after, result, summed_y):
    rows_x, rows_y, depth = own.shape
    for row in range(rows_x):
        summed_y[row] = along_y(taps, before_y, own, after_y, row)

    def layer(index):
        if index < 4:
            return before[index]
        return summed_y[index - 4] if index < 4 + rows_x else after[index - 4 - rows_x]

    for row in range(rows_x):
        summed = taps[0, 0, 0] * layer(row)
        for tap in range(1, 9):
            summed = summed + taps[0, 0, tap] * layer(row + tap)
        total = taps[2, 0, 4] * summed
        for tap in (0, 1, 2, 3, 5, 6, 7, 8):
            total = total + taps[2, 0, tap] * pltpu.roll(summed, (4 - tap) % depth, 1)
        result[row] = total


def in_vmem(count):
    return [pl.BlockSpec(memory_space=pltpu.VMEM)] * count


scalars = pl.BlockSpec(memory_space=pltpu.SMEM)
far = pl.BlockSpec(memory_space=pltpu.HBM)


def shape_of(*shape, dtype=jnp.float32):
    return jax.ShapeDtypeStruct(shape, dtype)


def call(kernel, outs, in_specs, scratch=(), out_specs=None, limit=16, flops=0, moved=0):
    if out_specs is None:
        out_specs = jax.tree.map(lambda _: pl.BlockSpec(memory_space=pltpu.VMEM), outs)
    return pl.pallas_call(
        kernel,
        out_shape=outs,
        in_specs=in_specs,
        out_specs=out_specs,
        scratch_shapes=list(scratch),
        compiler_params=pltpu.CompilerParams(vmem_limit_bytes=limit * 2**20),
        cost_estimate=pl.CostEstimate(flops=flops, bytes_accessed=moved, transcendentals=0),
    )


def per_device(charges, kernel_taps):
    count_x, count_y = lax.axis_size("gx"), lax.axis_size("gy")
    rows_x, rows_y, depth = charges.shape
    taps = jnp.transpose(kernel_taps, (1, 0, 2))
    both = ("gx", "gy")
    down, up = restrict_1d(0), prolong_1d(0)
    down_constants = np.concatenate(
        [
            padded(np.kron(down, down), lanes, rows_x * rows_y),
            restrict_window(lanes, 512, 128),
            restrict_window(lanes, 384, 64),
        ],
        axis=1,
    )
    down_constants = jnp.asarray(down_constants, jnp.bfloat16)

    up_1 = padded(np.kron(up, up), rows_x * rows_y, lanes)
    up_constants = jnp.asarray(
        np.concatenate([up_1, up_1, prolong_window(256, 256, 64)], axis=1), jnp.bfloat16
    )
    twice_up = jnp.asarray(prolong_ring(4 * lanes) @ prolong_ring(2 * lanes), jnp.bfloat16)
    sections, section_count = weight_sections(count_x, count_y)
    block_shape = (lanes * rows_per_block, lanes)
    exchange_shape = (lanes * rows_per_block, 1, lanes)

    blocks, head, tail = call(
        restrict_kernel,
        (
            shape_of(*block_shape),
            shape_of(rows_x, 4, depth),
            shape_of(rows_x, 4, depth),
        ),
        [far] * 3,
        [
            pltpu.SMEM(taps.shape, jnp.float32),
            pltpu.VMEM((rows_x, rows_y, depth), jnp.float32),
            pltpu.VMEM(down_constants.shape, jnp.bfloat16),
            pltpu.VMEM((2 * lanes, depth + 2 * lanes), jnp.bfloat16),
            pltpu.VMEM((7 * lanes + 48, lanes), jnp.float32),
            pltpu.VMEM(block_shape, jnp.float32),
            pltpu.SemaphoreType.DMA((9 + depth // 256,)),
        ],
        (far,) * 3,
        limit=60,
        flops=10**9,
        moved=2 * 10**6,
    )(taps, charges, down_constants)
    received = lax.all_to_all(blocks.reshape(exchange_shape), both, 0, 0, tiled=True)

    weights = call(
        lambda *refs: weight_kernel(sections, *refs),
        shape_of(section_count * lanes, 2 * lanes, dtype=jnp.bfloat16),
        [scalars] + in_vmem(1),
        flops=2 * 10**7,
        moved=3 * 10**6,
    )(taps, tap_tables())

    def shifted(values, axis, step):
        count = lax.axis_size(axis)
        return lax.ppermute(values, axis, [(i, (i + step) % count) for i in range(count)])

    before = shifted(tail, "gy", 1)
    after = shifted(head, "gy", -1)
    head, tail = call(
        edge_kernel,
        (shape_of(4, rows_y, depth), shape_of(4, rows_y, depth)),
        [scalars] + in_vmem(3),
        flops=10**11,
        moved=3 * 10**6,
    )(taps, before, charges, after)
    received, _ = lax.optimization_barrier((received, tail))
    finest = call(
        finest_kernel,
        shape_of(rows_x, rows_y, depth),
        [scalars] + in_vmem(5),
        [pltpu.VMEM((rows_x, rows_y, depth), jnp.float32)],
        flops=10**11,
        moved=3 * 10**6,
    )(taps, before, charges, after, shifted(tail, "gx", 1), shifted(head, "gx", -1))

    blocks = call(
        lambda *refs: convolve_kernel(sections, count_x, count_y, *refs),
        shape_of(*block_shape),
        in_vmem(2),
        [pltpu.VMEM(block_shape, jnp.float32), pltpu.SemaphoreType.DMA((4,))],
        far,
        flops=10**9,
        moved=4 * 10**6,
    )(received.reshape(block_shape), weights)
    received = lax.all_to_all(blocks.reshape(exchange_shape), both, 0, 0, tiled=True)

    return call(
        finish_kernel,
        shape_of(rows_x, rows_y, depth),
        in_vmem(4),
        [pltpu.VMEM((rows_x, rows_y, depth), jnp.float32), pltpu.SemaphoreType.DMA((depth // 256,))],
        far,
        flops=10**9,
        moved=4 * 10**6,
    )(received.reshape(block_shape), up_constants, twice_up, finest)


def solution(mesh):
    placed = (P("gx", "gy", None), P())
    return jax.shard_map(
        per_device, mesh=mesh, in_specs=placed, out_specs=P("gx", "gy", None), check_vma=False
    )
```

```python
import jax
import jax.numpy as jnp
import numpy as np
from jax import lax
from jax.experimental import pallas as pl
from jax.experimental.pallas import tpu as pltpu
from jax.sharding import PartitionSpec as P

first_cell = (0, -1, -2, -2)
cell_count = (16, 11, 9, 7)
brick_cells = (16, 8, 4, 2)
restrict_taps = {-3: -0.0625, -1: 0.5625, 0: 1.0, 1: 0.5625, 3: -0.0625}
lanes = 128
block_rows = ((), (0, 1, 2, 3), (4, 5), (6,))
rows_per_block = 7


def restrict_1d(level):
    matrix = np.zeros((cell_count[level + 1], cell_count[level]), np.float32)
    for coarse in range(cell_count[level + 1]):
        for fine in range(cell_count[level]):
            offset = first_cell[level] + fine - 2 * (first_cell[level + 1] + coarse)
            matrix[coarse, fine] = restrict_taps.get(offset, 0.0)
    return matrix


def prolong_entries(fine):
    if fine % 2 == 0:
        return {fine // 2: 1.0}
    left = (fine - 1) // 2
    return {left - 1: -0.0625, left: 0.5625, left + 1: 0.5625, left + 2: -0.0625}


def prolong_1d(level):
    matrix = np.zeros((cell_count[level], cell_count[level + 1]), np.float32)
    for fine in range(cell_count[level]):
        for coarse, weight in prolong_entries(first_cell[level] + fine).items():
            matrix[fine, coarse - first_cell[level + 1]] = weight
    return matrix


def padded(matrix, rows, columns):
    result = np.zeros((rows, columns), np.float32)
    result[: matrix.shape[0], : matrix.shape[1]] = matrix
    return result


def restrict_window(rows, width, margin):
    matrix = np.zeros((rows, width), np.float32)
    for coarse in range(rows):
        for offset, weight in restrict_taps.items():
            matrix[coarse, margin + 2 * coarse + offset] = weight
    return matrix


def prolong_window(rows, width, margin):
    matrix = np.zeros((rows, width), np.float32)
    for fine in range(rows):
        for coarse, weight in prolong_entries(fine).items():
            matrix[fine, margin + coarse] = weight
    return matrix


def prolong_ring(rows):
    matrix = np.zeros((rows, rows // 2), np.float32)
    for fine in range(rows):
        for coarse, weight in prolong_entries(fine).items():
            matrix[fine, coarse % (rows // 2)] = weight
    return matrix


def to_level(level):
    down = up = np.eye(cell_count[1], dtype=np.float32)
    for step in range(1, level):
        down, up = restrict_1d(step) @ down, up @ prolong_1d(step)
    return down, up


def tap_tables():
    count = cell_count[1]
    cells = [divmod(cell, count) for cell in range(count * count)]
    tables = []
    for axis in (0, 1):
        same = np.zeros((lanes, lanes), np.float32)
        for row, here in enumerate(cells):
            for column, there in enumerate(cells):
                same[row, column] = here[1 - axis] == there[1 - axis]
        tables.append(same)
    for level in (1, 2, 3):
        down, up = to_level(level)
        size = cell_count[level]
        for axis in (0, 1):
            into, out_of = np.zeros((lanes, lanes), np.float32), np.zeros((16, lanes), np.float32)
            number = np.full((16, lanes), 256.0, np.float32)
            for cell, place in enumerate(cells):
                into[cell, :size] = down[:, place[axis]]
                out_of[:size, cell] = up[place[axis], :]
            for source in range(size):
                for wanted in range(size):
                    number[source, wanted] = source - wanted + 4
            tables += [into, out_of, number]
    return jnp.asarray(np.concatenate(tables), jnp.bfloat16)


def brick_offsets(level, axis, bricks):
    if level == 3 and axis == 0:
        return tuple(range(bricks))
    reach = {1: 1, 2: 3, 3: 5}[level]
    return tuple(range(-reach, reach + 1))


def weight_sections(count_x, count_y):
    sections, start = {}, 0
    for level in (1, 2, 3):
        for axis, bricks in ((0, count_x), (1, count_y)):
            offsets = brick_offsets(level, axis, bricks)
            sections[level, axis] = (start, offsets)
            start += len(offsets)
    return sections, start


def split(values):
    high = values.astype(jnp.bfloat16)
    return high, (values - high.astype(jnp.float32)).astype(jnp.bfloat16)


def dot(left, right):
    return lax.dot_general(left, right, (((1,), (0,)), ((), ())), preferred_element_type=jnp.float32)


def dot_lanes(left, right):
    return lax.dot_general(left, right, (((1,), (1,)), ((), ())), preferred_element_type=jnp.float32)


def wrapped(values, margin, axis):
    size = values.shape[axis]
    tail = lax.slice_in_dim(values, size - margin, size, axis=axis)
    head = lax.slice_in_dim(values, 0, margin, axis=axis)
    return jnp.concatenate([tail, values, head], axis=axis)


def both_ways(product):
    half = product.shape[1] // 2
    return product[:, :half] + product[:, half:]


def side_by_side(values):
    return jnp.concatenate(split(values), axis=1)


def restrict_kernel(
    taps_far, charges_far, constants_far, blocks_far, head, tail, taps, charges, constants, patch, rim, blocks, arrived
):
    rows_x, rows_y, depth = charges.shape
    columns = rows_x * rows_y
    copies = [
        pltpu.make_async_copy(constants_far, constants, arrived.at[0]),
        pltpu.make_async_copy(taps_far, taps, arrived.at[1]),
    ]
    leaving = [
        pltpu.make_async_copy(charges.at[:, pl.ds(0, 4)], head, arrived.at[2]),
        pltpu.make_async_copy(charges.at[:, pl.ds(rows_y - 4, 4)], tail, arrived.at[3]),
    ]
    chunks = []
    for index in range(depth // 256):
        section = pl.ds(256 * index, 256)
        chunks.append(
            pltpu.make_async_copy(
                charges_far.at[:, :, section], charges.at[:, :, section], arrived.at[4 + index]
            )
        )
    copies[0].start()
    for chunk in chunks:
        chunk.start()
    copies[1].start()
    copies[0].wait()
    for index, chunk in enumerate(chunks):
        chunk.wait()
        high, low = split(charges[:, :, 256 * index : 256 * (index + 1)].reshape(columns, 256))
        down = constants[:, 0:columns]
        high, low = split(dot(down, high) + dot(down, low))
        begin = lanes + 256 * index
        patch[0:lanes, begin : begin + 256] = high
        patch[lanes : 2 * lanes, begin : begin + 256] = low
    for copy in leaving:
        copy.start()
    patch[:, 0:lanes] = patch[:, depth : depth + lanes]
    patch[:, depth + lanes : depth + 2 * lanes] = patch[:, lanes : 2 * lanes]
    lane_window = constants[:, 256:768]
    row_window = constants[:, 768:1152]
    grid = jnp.concatenate(
        [
            both_ways(dot_lanes(lane_window, patch[:, begin : begin + 512]))
            for begin in range(0, depth, 256)
        ],
        axis=0,
    )
    grids = {1: grid}
    for level in (1, 2):
        ready = wrapped(side_by_side(grid), 64, 0)
        grid = jnp.concatenate(
            [
                both_ways(dot(row_window, ready[begin : begin + 384]))
                for begin in range(0, grid.shape[0], 256)
            ],
            axis=0,
        )
        grids[level + 1] = grid
    copies[1].wait()
    firsts, first = {}, 0
    for level in (1, 2, 3):
        grid = grids[level]
        cells = grid.shape[0]
        rim[first : first + 8, :] = grid[cells - 8 :, :]
        rim[first + 8 : first + 8 + cells, :] = grid
        rim[first + 8 + cells : first + 16 + cells, :] = grid[:8, :]
        firsts[level] = first
        first += cells + 16
    share = lanes // 4
    for part in range(4):
        for level in (1, 2, 3):
            for index, row in enumerate(block_rows[level]):
                summed = None
                for tap in range(9):
                    begin = firsts[level] + lanes * index + share * part + 4 + tap
                    term = taps[2, level, tap] * rim[begin : begin + share, :]
                    summed = term if summed is None else summed + term
                blocks[pl.ds(rows_per_block * share * part + row, share, stride=rows_per_block), :] = summed
        section = pl.ds(rows_per_block * share * part, rows_per_block * share)
        leaving.append(
            pltpu.make_async_copy(blocks.at[section], blocks_far.at[section], arrived.at[4 + depth // 256 + part])
        )
        leaving[-1].start()
    for copy in leaving:
        copy.wait()


def weight_kernel(sections, taps, tables, weights):
    tables_at = {
        (level, axis): 2 * lanes + (2 * (level - 1) + axis) * (lanes + 32) for level, axis in sections
    }
    stacks = {}
    for (level, axis), (start, offsets) in sections.items():
        begin = tables_at[level, axis] + lanes + 16
        base = tables[begin : begin + 16, :].astype(jnp.float32).astype(jnp.int32)
        scale = 0.5**level if axis == 0 else 1.0
        values = [scale * taps[axis, level, tap] for tap in range(9)]
        stack = []
        for offset in offsets:
            number = base + brick_cells[level] * offset
            if level == 3 and axis == 0:
                number = number & 271
            chosen = jnp.zeros(number.shape, jnp.float32)
            for tap in range(9):
                chosen = jnp.where(number == tap, values[tap], chosen)
            stack.append(chosen)
        stacks[level, axis] = split(jnp.concatenate(stack, axis=0))
    for level, axis in sections:
        begin = tables_at[level, axis] + lanes
        high, low = stacks[level, axis]
        out_of = tables[begin : begin + 16, :]
        stacks[level, axis] = split(dot(high[:, 0:16], out_of) + dot(low[:, 0:16], out_of))
    for (level, axis), (start, offsets) in sections.items():
        same = tables[axis * lanes : (axis + 1) * lanes, :].astype(jnp.float32)
        into = tables[tables_at[level, axis] : tables_at[level, axis] + lanes, 0:16]
        into = jnp.concatenate([into, into], axis=1)
        for index in range(0, len(offsets), 2):
            pair = range(index, min(index + 2, len(offsets)))
            parts = [
                jnp.concatenate([half[16 * part : 16 * (part + 1)] for part in pair], axis=1)
                for half in stacks[level, axis]
            ]
            spread = dot(into, jnp.concatenate(parts, axis=0))
            for place, part in enumerate(pair):
                rows = pl.ds((start + part) * lanes, lanes)
                weights[rows, :] = side_by_side(spread[:, place * lanes : (place + 1) * lanes] * same)


def weighted(pieces, weights, start):
    rows = pl.ds(start * lanes, len(pieces) * lanes)
    product = both_ways(dot(jnp.concatenate(pieces, axis=1), weights[rows, :]))
    half = product.shape[0] // 2
    return product[:half] + product[half:]


def convolve_kernel(sections, count_x, count_y, received, weights, blocks_far, blocks, left):
    columns = {}
    for level in (1, 2, 3):
        slices = len(block_rows[level])
        values = jnp.concatenate(
            [received[pl.ds(row, lanes, stride=rows_per_block), :] for row in block_rows[level]], axis=0
        )
        start, offsets = sections[level, 0]
        stack = jnp.concatenate(split(values), axis=0).reshape(2 * slices, count_x, count_y, lanes)
        pieces = []
        for offset in offsets:
            turn = offset % count_x
            turned = jnp.concatenate([stack[:, turn:], stack[:, :turn]], axis=1) if turn else stack
            pieces.append(turned.reshape(2 * slices * lanes, lanes))
        columns[level] = weighted(pieces, weights, start)
    for level in (1, 2, 3):
        slices = len(block_rows[level])
        start, offsets = sections[level, 1]
        stack = columns[level].reshape(slices * count_x, count_y, lanes)
        pieces = []
        for offset in offsets:
            turn = offset % count_y
            turned = jnp.concatenate([stack[:, turn:], stack[:, :turn]], axis=1) if turn else stack
            pieces.append(jnp.concatenate(split(turned.reshape(slices * lanes, lanes)), axis=0))
        values = weighted(pieces, weights, start)
        for index, row in enumerate(block_rows[level]):
            blocks[pl.ds(row, lanes, stride=rows_per_block), :] = values[lanes * index : lanes * (index + 1)]
    copies = []
    for index in range(4):
        section = pl.ds(224 * index, 224)
        copies.append(pltpu.make_async_copy(blocks.at[section], blocks_far.at[section], left.at[index]))
        copies[-1].start()
    for copy in copies:
        copy.wait()


def finish_kernel(received, constants, twice_up, finest, potential, ready, left):
    rows_x, rows_y, depth = finest.shape
    row_window = constants[:, 256:512]
    parts = {
        level: jnp.concatenate(
            [received[pl.ds(row, lanes, stride=rows_per_block), :] for row in block_rows[level]], axis=0
        )
        for level in (1, 2, 3)
    }
    coarsest = both_ways(dot(twice_up[...], side_by_side(parts[3])))
    pairs = wrapped(side_by_side(parts[2]), 64, 0)
    middle = jnp.concatenate(
        [both_ways(dot(row_window, pairs[begin : begin + 256])) for begin in (0, lanes)], axis=0
    )
    running = parts[1] + middle + coarsest
    pairs = wrapped(side_by_side(running), 64, 0)
    fines = [
        side_by_side(both_ways(dot(row_window, pairs[lanes * index : lanes * index + 256])))
        for index in range(depth // 256)
    ]
    copies = []
    for index, fine in enumerate(fines):
        smooth = dot_lanes(constants[:, 0:256], fine)
        section = slice(256 * index, 256 * (index + 1))
        ready[:, :, section] = finest[:, :, section] + smooth.reshape(rows_x, rows_y, 256)
        places = pl.ds(256 * index, 256)
        copies.append(
            pltpu.make_async_copy(ready.at[:, :, places], potential.at[:, :, places], left.at[index])
        )
        copies[-1].start()
    for copy in copies:
        copy.wait()


def along_y(taps, before, own, after, row):
    rows_y = own.shape[1]
    lines = jnp.concatenate([before[row], own[row], after[row]], axis=0)
    summed = taps[1, 0, 0] * lines[0:rows_y]
    for tap in range(1, 9):
        summed = summed + taps[1, 0, tap] * lines[tap : tap + rows_y]
    return summed


def edge_kernel(taps, before, own, after, head, tail):
    rows_x = own.shape[0]
    for row in range(4):
        head[row] = along_y(taps, before, own, after, row)
        tail[row] = along_y(taps, before, own, after, rows_x - 4 + row)


def finest_kernel(taps, before_y, own, after_y, before, after, result, summed_y):
    rows_x, rows_y, depth = own.shape
    for row in range(rows_x):
        summed_y[row] = along_y(taps, before_y, own, after_y, row)

    def layer(index):
        if index < 4:
            return before[index]
        return summed_y[index - 4] if index < 4 + rows_x else after[index - 4 - rows_x]

    for row in range(rows_x):
        summed = taps[0, 0, 0] * layer(row)
        for tap in range(1, 9):
            summed = summed + taps[0, 0, tap] * layer(row + tap)
        total = taps[2, 0, 4] * summed
        for tap in (0, 1, 2, 3, 5, 6, 7, 8):
            total = total + taps[2, 0, tap] * pltpu.roll(summed, (4 - tap) % depth, 1)
        result[row] = total


def in_vmem(count):
    return [pl.BlockSpec(memory_space=pltpu.VMEM)] * count


scalars = pl.BlockSpec(memory_space=pltpu.SMEM)
far = pl.BlockSpec(memory_space=pltpu.HBM)


def shape_of(*shape, dtype=jnp.float32):
    return jax.ShapeDtypeStruct(shape, dtype)


def call(kernel, outs, in_specs, scratch=(), out_specs=None, limit=16, flops=0, moved=0):
    if out_specs is None:
        out_specs = jax.tree.map(lambda _: pl.BlockSpec(memory_space=pltpu.VMEM), outs)
    return pl.pallas_call(
        kernel,
        out_shape=outs,
        in_specs=in_specs,
        out_specs=out_specs,
        scratch_shapes=list(scratch),
        compiler_params=pltpu.CompilerParams(vmem_limit_bytes=limit * 2**20),
        cost_estimate=pl.CostEstimate(flops=flops, bytes_accessed=moved, transcendentals=0),
    )


def per_device(charges, kernel_taps):
    count_x, count_y = lax.axis_size("gx"), lax.axis_size("gy")
    rows_x, rows_y, depth = charges.shape
    taps = jnp.transpose(kernel_taps, (1, 0, 2))
    both = ("gx", "gy")
    down, up = restrict_1d(0), prolong_1d(0)
    down_constants = np.concatenate(
        [
            padded(np.kron(down, down), lanes, rows_x * rows_y),
            restrict_window(lanes, 512, 128),
            restrict_window(lanes, 384, 64),
        ],
        axis=1,
    )
    down_constants = jnp.asarray(down_constants, jnp.bfloat16)

    up_1 = padded(np.kron(up, up), rows_x * rows_y, lanes)
    up_constants = jnp.asarray(
        np.concatenate([up_1, up_1, prolong_window(256, 256, 64)], axis=1), jnp.bfloat16
    )
    twice_up = jnp.asarray(prolong_ring(4 * lanes) @ prolong_ring(2 * lanes), jnp.bfloat16)
    sections, section_count = weight_sections(count_x, count_y)
    block_shape = (lanes * rows_per_block, lanes)
    exchange_shape = (lanes * rows_per_block, 1, lanes)

    blocks, head, tail = call(
        restrict_kernel,
        (
            shape_of(*block_shape),
            shape_of(rows_x, 4, depth),
            shape_of(rows_x, 4, depth),
        ),
        [far] * 3,
        [
            pltpu.SMEM(taps.shape, jnp.float32),
            pltpu.VMEM((rows_x, rows_y, depth), jnp.float32),
            pltpu.VMEM(down_constants.shape, jnp.bfloat16),
            pltpu.VMEM((2 * lanes, depth + 2 * lanes), jnp.bfloat16),
            pltpu.VMEM((7 * lanes + 48, lanes), jnp.float32),
            pltpu.VMEM(block_shape, jnp.float32),
            pltpu.SemaphoreType.DMA((8 + depth // 256,)),
        ],
        (far,) * 3,
        limit=60,
        flops=10**9,
        moved=2 * 10**6,
    )(taps, charges, down_constants)
    received = lax.all_to_all(blocks.reshape(exchange_shape), both, 0, 0, tiled=True)

    weights = call(
        lambda *refs: weight_kernel(sections, *refs),
        shape_of(section_count * lanes, 2 * lanes, dtype=jnp.bfloat16),
        [scalars] + in_vmem(1),
        flops=2 * 10**7,
        moved=3 * 10**6,
    )(taps, tap_tables())

    def shifted(values, axis, step):
        count = lax.axis_size(axis)
        return lax.ppermute(values, axis, [(i, (i + step) % count) for i in range(count)])

    before = shifted(tail, "gy", 1)
    after = shifted(head, "gy", -1)
    head, tail = call(
        edge_kernel,
        (shape_of(4, rows_y, depth), shape_of(4, rows_y, depth)),
        [scalars] + in_vmem(3),
        flops=10**11,
        moved=3 * 10**6,
    )(taps, before, charges, after)
    received, _ = lax.optimization_barrier((received, tail))
    finest = call(
        finest_kernel,
        shape_of(rows_x, rows_y, depth),
        [scalars] + in_vmem(5),
        [pltpu.VMEM((rows_x, rows_y, depth), jnp.float32)],
        flops=10**11,
        moved=3 * 10**6,
    )(taps, before, charges, after, shifted(tail, "gx", 1), shifted(head, "gx", -1))

    blocks = call(
        lambda *refs: convolve_kernel(sections, count_x, count_y, *refs),
        shape_of(*block_shape),
        in_vmem(2),
        [pltpu.VMEM(block_shape, jnp.float32), pltpu.SemaphoreType.DMA((4,))],
        far,
        flops=10**9,
        moved=4 * 10**6,
    )(received.reshape(block_shape), weights)
    received = lax.all_to_all(blocks.reshape(exchange_shape), both, 0, 0, tiled=True)

    return call(
        finish_kernel,
        shape_of(rows_x, rows_y, depth),
        in_vmem(4),
        [pltpu.VMEM((rows_x, rows_y, depth), jnp.float32), pltpu.SemaphoreType.DMA((depth // 256,))],
        far,
        flops=10**9,
        moved=4 * 10**6,
    )(received.reshape(block_shape), up_constants, twice_up, finest)


def solution(mesh):
    placed = (P("gx", "gy", None), P())
    return jax.shard_map(
        per_device, mesh=mesh, in_specs=placed, out_specs=P("gx", "gy", None), check_vma=False
    )
```
